128 devices in a mesh: row: 8 (over x, z_lo), col: 16 (over z_hi, y, core).
Axes of the slice: x: 4, y: 4, z: 4 (z_hi: 2, z_lo: 2; z = z_hi * 2 + z_lo), core: 2. Of those that a mesh axis runs over, the one named last changes fastest.
Arguments:
- object_field: float32 [2, 4096, 8192], P(None, 'row', 'col'), may hold values from -5 to 5
- probe: float32 [2, 256, 256], replicated, may hold values from -6 to 6
- intensity: float32 [1536, 256, 256], P(('row', 'col')), may hold values from 0 to 4
- centers: int32 [1536, 2], P(('row', 'col')), may hold values from 0 to 8191, as said below
- picked: int32 [1536], P(('row', 'col')), may hold values 0 or 1
Outputs:
- object_out: float32 [2, 4096, 8192], P(None, 'row', 'col')
- probe_out: float32 [2, 256, 256], replicated
The draws below stay inside these ranges and needn't reach their ends.
Inputs may be any that keep to these rules, and one draw needn't show every extreme that they name: `centers`: the frames f with k * 12 <= f < (k + 1) * 12 belong to subdomain k = 16 i + j: their centres lie in rows i * 512 to (i + 1) * 512 - 1 and columns j * 512 to (j + 1) * 512 - 1. Of one subdomain's frames at most 6 have centres in any one quarter of it (upper or lower 512/2 rows times left or right 512/2 columns), and in every subdomain some quarter holds exactly 6.
All inputs are finite; a program needn't handle non-finite values. No bound on the sum of `picked` on one device may be relied on, other than what follows from the above.
Results may differ from the reference program's by a relative error of at most 0.012.
The reference program's roundings to bfloat16 on the way count: a program that leaves them out, or rounds other values in their place, can miss the bound.
Values sent between devices are 32-bit elements; how exact they have to be, the bound alone decides.
No kernel may reach another device: no remote copies, remote signals or barrier semaphores. Data moves between devices by JAX's collectives and lax.ppermute only.
A program may use at most 128 MiB of HBM per device.

```python
import math
import jax
import jax.numpy as jnp
from jax import lax

P_SIZE = 256
S = 512
FD = 12
ITERS = 2
CAP = 6
FRAMES = 1536
NR = 4096
NC = 8192
N_COL = 16


def draw_centers(key, part):
    key = jax.random.fold_in(key, 11)
    device_count = FRAMES // FD
    key_main, key_other, key_order, key_offset = jax.random.split(key, 4)
    main_quarter = jax.random.randint(key_main, (device_count, 1), 0, 4)
    other_quarter = (main_quarter + 1 + jax.random.randint(key_other, (device_count, CAP), 0, 3)) % 4
    quarters = jnp.concatenate([jnp.broadcast_to(main_quarter, (device_count, CAP)), other_quarter], axis=1)
    order_keys = jax.random.split(key_order, device_count)
    orders = jax.vmap(lambda single: jax.random.permutation(single, FD))(order_keys)
    quarters = jnp.take_along_axis(quarters, orders, axis=1)
    offsets = jax.random.randint(key_offset, (device_count, FD, 2), 0, S // 2)
    devices = jnp.arange(device_count, dtype=jnp.int32)
    row_start = devices // N_COL * S
    col_start = devices % N_COL * S
    rows_here = row_start[:, None] + quarters // 2 * (S // 2) + offsets[..., 0]
    cols_here = col_start[:, None] + quarters % 2 * (S // 2) + offsets[..., 1]
    return jnp.stack([rows_here, cols_here], axis=-1).reshape(FRAMES, 2).astype(jnp.int32)


def set_ends(values, key, low, top_value):
    spot = [jax.random.randint(jax.random.fold_in(key, axis), (), 0, length) for axis, length in enumerate(values.shape)]
    widest = values.shape.index(max(values.shape))
    beside = spot[:widest] + [(spot[widest] + 1) % values.shape[widest]] + spot[widest + 1:]
    return values.at[tuple(spot)].set(low).at[tuple(beside)].set(top_value)


def levels(rng, extent, pieces, low, top_value):
    def one(position, parts):
        draws = jax.random.uniform(jax.random.fold_in(jax.random.fold_in(rng, 6), position), (parts,), jnp.float32, low / len(pieces), top_value / len(pieces))
        return jnp.repeat(jnp.exp(draws), extent[position] // parts).reshape((-1,) + (1,) * (len(extent) - position - 1))

    gain = one(*pieces[0])
    for cut in pieces[1:]:
        gain = gain * one(*cut)
    return gain


def normal_values(stream_key, dims, spread, bound, cuts=(), kind=jnp.bfloat16):
    drawn = jax.random.normal(stream_key, dims, jnp.float32) * spread
    if len(cuts) > 0:
        drawn = levels(stream_key, dims, cuts, -0.22, 0.18) * drawn
    return jnp.clip(drawn, min=-bound, max=bound).astype(kind)


def setup_inputs(seed: int = 0) -> dict:
    arg_keys = jax.random.split(jax.random.key(seed), 6)
    return {
        "object_field": normal_values(arg_keys[0], (2, NR, NC), 0.7, 5.0, ((1, 8), (2, 16)), jnp.float32),
        "probe": normal_values(arg_keys[1], (2, P_SIZE, P_SIZE), 1.0, 6.0, (), jnp.float32),
        "intensity": jnp.clip(4.0 * jax.random.uniform(arg_keys[2], (FRAMES, P_SIZE, P_SIZE), jnp.float32) ** levels(arg_keys[2], (FRAMES, P_SIZE, P_SIZE), ((0, 128),), -0.2, 0.2), 0.0, 4.0),
        "centers": draw_centers(jax.random.fold_in(arg_keys[5], 71), 0),
        "picked": set_ends((jax.random.randint(arg_keys[4], (FRAMES,), 0, 4) < 3).astype(jnp.int32), jax.random.fold_in(arg_keys[4], 1), 0, 1),
    }


object_rate = 0.02
probe_gain = 4.0

def tables(frame_side):
    indices = jnp.arange(frame_side, dtype=jnp.int32)
    product = indices[:, None] * indices[None, :] % frame_side
    angle = product.astype(jnp.float32) * (2.0 * math.pi / frame_side)
    scale = 1.0 / math.sqrt(frame_side)
    real_part = (jnp.cos(angle) * scale).astype(jnp.bfloat16)
    imag_part = (-jnp.sin(angle) * scale).astype(jnp.bfloat16)
    right_mat = jnp.concatenate([jnp.concatenate([real_part, imag_part], 1), jnp.concatenate([-imag_part, real_part], 1)], 0)
    left_mat = jnp.concatenate([jnp.concatenate([real_part, -imag_part], 1), jnp.concatenate([imag_part, real_part], 1)], 0)
    return (right_mat, left_mat)

def frame_terms(windows, probe_now, intens, chosen, right_mat, left_mat):
    frame_side = probe_now.shape[-1]
    right_full = right_mat.astype(jnp.float32)
    left_full = left_mat.astype(jnp.float32)
    probe_re, probe_im = (probe_now[0], probe_now[1])
    window_re, window_im = (windows[:, 0], windows[:, 1])
    exit_re = probe_re * window_re - probe_im * window_im
    exit_im = probe_re * window_im + probe_im * window_re
    flat_exit = jnp.concatenate([exit_re, exit_im], axis=2).astype(jnp.bfloat16).astype(jnp.float32)
    partial_wave = jnp.einsum('nab,bc->nac', flat_exit, right_full).astype(jnp.bfloat16).astype(jnp.float32)
    stacked = jnp.concatenate([partial_wave[:, :, :frame_side], partial_wave[:, :, frame_side:]], axis=1)
    farfield = jnp.einsum('ab,nbc->nac', left_full, stacked)
    far_re, far_im = (farfield[:, :frame_side], farfield[:, frame_side:])
    mismatch = (far_re * far_re + far_im * far_im - intens) * chosen.astype(jnp.float32)[:, None, None]
    weighted = jnp.concatenate([mismatch * far_re, mismatch * far_im], axis=1).astype(jnp.bfloat16).astype(jnp.float32)
    returned = jnp.einsum('ab,nbc->nac', right_full, weighted).astype(jnp.bfloat16).astype(jnp.float32)
    flat_back = jnp.concatenate([returned[:, :frame_side], returned[:, frame_side:]], axis=2)
    gradient = jnp.einsum('nab,bc->nac', flat_back, left_full)
    grad_re, grad_im = (gradient[..., :frame_side], gradient[..., frame_side:])
    object_re = probe_re * grad_re + probe_im * grad_im
    object_im = probe_re * grad_im - probe_im * grad_re
    probe_re_sum = lax.optimization_barrier(jnp.sum(window_re * grad_re + window_im * grad_im, axis=0))
    probe_im_sum = lax.optimization_barrier(jnp.sum(window_re * grad_im - window_im * grad_re, axis=0))
    return (jnp.stack([object_re, object_im], axis=1), jnp.stack([probe_re_sum, probe_im_sum]))

def reference(object_field, probe, intensity, centers, picked):
    frame_side = probe.shape[-1]
    rows_all = object_field.shape[1]
    cols_all = object_field.shape[2]
    right_mat, left_mat = tables(frame_side)
    batch_rows = 4 * FD
    batch_count = FRAMES // batch_rows
    offsets = jnp.arange(frame_side, dtype=jnp.int32) - frame_side // 2
    object_now = object_field
    probe_now = probe
    for sweep in range(ITERS):

        def one_batch(carried, batch_at):
            object_grad, probe_grad = carried
            start = (batch_at * batch_rows).astype(jnp.int32)
            batch_centers = lax.dynamic_slice_in_dim(centers, start, batch_rows, 0)
            batch_intens = lax.dynamic_slice_in_dim(intensity, start, batch_rows, 0)
            batch_picked = lax.dynamic_slice_in_dim(picked, start, batch_rows, 0)
            row_ids = (batch_centers[:, 0:1] + offsets[None, :]) % rows_all
            col_ids = (batch_centers[:, 1:2] + offsets[None, :]) % cols_all
            windows = jnp.moveaxis(object_now[:, row_ids[:, :, None], col_ids[:, None, :]], 0, 1)
            contrib, probe_part = frame_terms(windows, probe_now, batch_intens, batch_picked, right_mat, left_mat)
            object_grad = object_grad.at[:, row_ids[:, :, None], col_ids[:, None, :]].add(jnp.moveaxis(contrib, 1, 0))
            return ((object_grad, probe_grad + probe_part), None)
        start_state = (jnp.zeros(object_now.shape, jnp.float32), jnp.zeros(probe_now.shape, jnp.float32))
        (object_grad, probe_grad), _ = lax.scan(one_batch, start_state, jnp.arange(batch_count, dtype=jnp.int32))
        object_now = object_now - object_rate * object_grad
        probe_now = probe_now - probe_gain / FRAMES * probe_grad
    moved = jnp.roll(object_now, (-(S // 2), -(S // 2)), axis=(1, 2))
    return (moved, probe_now)
```

```python
import math

import jax
import jax.numpy as jnp
import numpy as np
from jax import lax
from jax.experimental import pallas as pl
from jax.experimental.pallas import tpu as pltpu
from jax.sharding import PartitionSpec as P

ITERS = 2


object_rate = 0.02
probe_gain = 4.0
LANES = 128
SUBLANES = 8


def tables(frame_side):
    indices = np.arange(frame_side)
    angle = (indices[:, None] * indices[None, :] % frame_side) * (2.0 * math.pi / frame_side)
    scale = 1.0 / math.sqrt(frame_side)
    real_part = (np.cos(angle) * scale).astype(np.float32).astype(jnp.bfloat16)
    imag_part = (-np.sin(angle) * scale).astype(np.float32).astype(jnp.bfloat16)
    right_mat = np.block([[real_part, imag_part], [-imag_part, real_part]])
    left_mat = np.block([[real_part, -imag_part], [imag_part, real_part]])
    return (jnp.asarray(right_mat), jnp.asarray(left_mat))


def frames_kernel(places, out_cols, side, info, *refs):
    count = len(places)
    pieces = refs[:count]
    probe, intens, right_mat, left_mat = refs[count : count + 4]
    outs = refs[count + 4 : count + 4 + len(out_cols)]
    probe_grad, region, grad, held, chosen = refs[count + 4 + len(out_cols) :]
    for piece, (row_at, col_at) in zip(pieces, places):
        rows, cols = piece.shape[1:]
        region[:, row_at : row_at + rows, col_at : col_at + cols] = piece[...]
    grad[...] = jnp.zeros_like(grad)
    probe_grad[...] = jnp.zeros_like(probe_grad)

    def pick(slot, found):
        @pl.when(info[slot, 2] != 0)
        def _():
            chosen[found] = slot

        return found + jnp.where(info[slot, 2] != 0, 1, 0)

    total = lax.fori_loop(0, info.shape[0], pick, jnp.int32(0))
    lane = lax.broadcasted_iota(jnp.int32, (side + SUBLANES, LANES), 1)
    line = lax.broadcasted_iota(jnp.int32, (1, SUBLANES, LANES), 1)

    def one_frame(at, carried):
        slot = chosen[at]
        row_at = info[slot, 0]
        col_at = info[slot, 1]
        col_base = pl.multiple_of(col_at // LANES * LANES, LANES)
        row_base = pl.multiple_of(row_at // SUBLANES * SUBLANES, SUBLANES)
        col_shift = col_at - col_base
        row_shift = row_at - row_base
        col_back = jnp.where(col_shift == 0, 0, LANES - col_shift)
        row_back = jnp.where(row_shift == 0, 0, SUBLANES - row_shift)
        rows = pl.ds(row_base, side + SUBLANES)
        tiles = side // SUBLANES
        inside = lane < LANES - col_shift
        inside_row = line < SUBLANES - row_shift

        def window(part):
            turned = [
                pltpu.roll(region[part, rows, pl.ds(pl.multiple_of(col_base + LANES * k, LANES), LANES)], col_back, 1)
                for k in range(3)
            ]
            for k in range(2):
                piece = jnp.where(inside, turned[k], turned[k + 1]).reshape(tiles + 1, SUBLANES, LANES)
                piece = pltpu.roll(piece, row_back, 1)
                piece = jnp.where(inside_row, piece[:tiles], piece[1:]).reshape(side, LANES)
                held[part, :, k * LANES : (k + 1) * LANES] = piece

        window(0)
        window(1)
        win_re, win_im = held[0], held[1]
        pr_re, pr_im = probe[0], probe[1]
        exit_re = pr_re * win_re - pr_im * win_im
        exit_im = pr_re * win_im + pr_im * win_re
        flat = jnp.concatenate([exit_re, exit_im], axis=1).astype(jnp.bfloat16)
        wave = jnp.dot(flat, right_mat[...], preferred_element_type=jnp.float32).astype(jnp.bfloat16)
        stacked = jnp.concatenate([wave[:, :side], wave[:, side:]], axis=0)
        far = jnp.dot(left_mat[...], stacked, preferred_element_type=jnp.float32)
        far_re, far_im = far[:side], far[side:]
        mismatch = far_re * far_re + far_im * far_im - intens[slot]
        weighted = jnp.concatenate([mismatch * far_re, mismatch * far_im], axis=0).astype(jnp.bfloat16)
        returned = jnp.dot(right_mat[...], weighted, preferred_element_type=jnp.float32).astype(jnp.bfloat16)
        flat_back = jnp.concatenate([returned[:side], returned[side:]], axis=1)
        gradient = jnp.dot(flat_back, left_mat[...], preferred_element_type=jnp.float32)
        gr_re, gr_im = gradient[:, :side], gradient[:, side:]
        win_re, win_im = held[0], held[1]
        probe_grad[0] += win_re * gr_re + win_im * gr_im
        probe_grad[1] += win_re * gr_im - win_im * gr_re
        outside = lane >= col_shift
        outside_row = line >= row_shift
        nothing = jnp.zeros((1, SUBLANES, LANES), jnp.float32)

        def spread(part, value):
            turned = []
            for k in range(2):
                piece = value[:, k * LANES : (k + 1) * LANES].reshape(tiles, SUBLANES, LANES)
                piece = pltpu.roll(piece, row_shift, 1)
                piece = jnp.where(
                    outside_row,
                    jnp.concatenate([piece, nothing], axis=0),
                    jnp.concatenate([nothing, piece], axis=0),
                ).reshape(side + SUBLANES, LANES)
                turned.append(pltpu.roll(piece, col_shift, 1))
            first, second = turned
            grad[part, rows, pl.ds(col_base, LANES)] += jnp.where(outside, first, 0.0)
            grad[part, rows, pl.ds(pl.multiple_of(col_base + LANES, LANES), LANES)] += jnp.where(outside, second, first)
            grad[part, rows, pl.ds(pl.multiple_of(col_base + 2 * LANES, LANES), LANES)] += jnp.where(outside, 0.0, second)

        spread(0, pr_re * gr_re + pr_im * gr_im)
        spread(1, pr_re * gr_im - pr_im * gr_re)
        return carried

    lax.fori_loop(0, total, one_frame, 0)
    for out, (first, last) in zip(outs, out_cols):
        out[...] = grad[:, :, first:last]


def frames(info, pieces, places, probe, intensity, mats, rows, cols, out_cols):
    side = probe.shape[-1]
    vmem = pl.BlockSpec(memory_space=pltpu.VMEM)
    smem = pl.BlockSpec(memory_space=pltpu.SMEM)
    out_shapes = [jax.ShapeDtypeStruct((2, rows, last - first), jnp.float32) for first, last in out_cols]
    out_shapes.append(jax.ShapeDtypeStruct(probe.shape, jnp.float32))

    def kernel(*refs):
        frames_kernel(places, out_cols, side, *refs)

    return pl.pallas_call(
        kernel,
        out_shape=out_shapes,
        in_specs=[smem] + [vmem] * (len(pieces) + 4),
        out_specs=[vmem] * len(out_shapes),
        scratch_shapes=[
            pltpu.VMEM((2, rows, cols), jnp.float32),
            pltpu.VMEM((2, rows, cols), jnp.float32),
            pltpu.VMEM(probe.shape, jnp.float32),
            pltpu.SMEM((info.shape[0],), jnp.int32),
        ],
        compiler_params=pltpu.CompilerParams(vmem_limit_bytes=56 * 1024 * 1024),
        name="frames",
    )(info, *pieces, probe, intensity, *mats)


def shifted(array, axis, by):
    count = lax.axis_size(axis)
    return lax.ppermute(array, axis, [(i, (i + by) % count) for i in range(count)])


def probe_sum(part, shape):
    row_count, col_count = lax.axis_size("row"), lax.axis_size("col")
    x_count, lo_count, core_count = row_count // 2, 2, 2
    y_count, hi_count = col_count // 4, 2
    z_count = lo_count * hi_count

    def place(x, z, y, core):
        return (x * lo_count + z % lo_count) * col_count + (z // lo_count) * (y_count * core_count) + y * core_count + core

    def moved(array, axis, by):
        pairs = []
        for x in range(x_count):
            for z in range(z_count):
                for y in range(y_count):
                    for core in range(core_count):
                        to = {"x": x, "z": z, "y": y, "core": core}
                        size = {"x": x_count, "z": z_count, "y": y_count, "core": core_count}[axis]
                        to[axis] = (to[axis] + by) % size
                        pairs.append((place(x, z, y, core), place(**to)))
        return lax.ppermute(array, ("row", "col"), pairs)

    col = lax.axis_index("col")
    core = col % core_count
    y = col // core_count % y_count
    flat = part.reshape(-1, shape[-1])
    halves = flat.reshape(core_count, -1, shape[-1])
    mine = lax.dynamic_index_in_dim(halves, core, 0, False)
    other = lax.dynamic_index_in_dim(halves, 1 - core, 0, False)
    mine = mine + moved(other, "core", 1)
    quarters = mine.reshape(y_count, -1, shape[-1])
    total = lax.dynamic_index_in_dim(quarters, y, 0, False)
    arrived = [
        moved(lax.dynamic_index_in_dim(quarters, (y + by) % y_count, 0, False), "y", by) for by in range(1, y_count)
    ]
    for value in arrived:
        total = total + value
    for axis, size in (("x", x_count), ("z", z_count)):
        arrived = [moved(total, axis, by) for by in range(1, size)]
        for value in arrived:
            total = total + value
    gathered = [total] + [moved(total, "y", by) for by in range(1, y_count)]
    half = jnp.zeros(quarters.shape, jnp.float32)
    for by, value in enumerate(gathered):
        half = lax.dynamic_update_index_in_dim(half, value, (y - by) % y_count, 0)
    half = half.reshape(mine.shape)
    other = moved(half, "core", 1)
    first = jnp.where(core == 0, half, other)
    second = jnp.where(core == 0, other, half)
    return jnp.concatenate([first, second], axis=0).reshape(shape)


def on_device(object_field, probe, intensity, centers, picked):
    tile = object_field.shape[1]
    side = probe.shape[-1]
    width = side // 2
    half = tile // 2
    full = tile + side
    rows_all = tile * lax.axis_size("row")
    cols_all = tile * lax.axis_size("col")
    frames_total = intensity.shape[0] * lax.axis_size("row") * lax.axis_size("col")
    mats = tables(side)
    local_row = (centers[:, 0] - lax.axis_index("row") * tile) % rows_all
    local_col = (centers[:, 1] - lax.axis_index("col") * tile) % cols_all
    info = jnp.stack([local_row, local_col, picked], axis=1)
    out_cols = ((0, width), (width, width + tile), (width + tile, full))

    below = shifted(object_field[:, :width], "row", -1)
    above = shifted(object_field[:, tile - width :], "row", 1)
    at_left = shifted(object_field[:, :, tile - width :], "col", 1)
    at_right = shifted(object_field[:, :, :width], "col", -1)
    ends = jnp.concatenate([above, below], axis=1)
    ends_left = shifted(ends[:, :, tile - width :], "col", 1)
    ends_right = shifted(ends[:, :, :width], "col", -1)
    left_old = jnp.concatenate([ends_left[:, :width], at_left, ends_left[:, width:]], axis=1)
    right_old = jnp.concatenate([ends_right[:, :width], at_right, ends_right[:, width:]], axis=1)
    centre_old = jnp.concatenate([above, object_field, below], axis=1)
    places = ((0, 0), (0, width), (0, width + tile))
    grad_left, grad_mid, grad_right, probe_part = frames(
        info, (left_old, centre_old, right_old), places, probe, intensity, mats, full, full, out_cols
    )

    probe_total = probe_sum(probe_part, probe.shape)
    from_right = shifted(grad_left, "col", -1)
    from_left = shifted(grad_right, "col", 1)
    inner_up = shifted(grad_mid[:, :side, width : tile - width], "row", -1)
    inner_down = shifted(grad_mid[:, tile:, width : tile - width], "row", 1)
    edge_left = grad_mid[:, :, :width] + from_left
    edge_right = grad_mid[:, :, tile - width :] + from_right
    edges = jnp.concatenate([edge_left, edge_right], axis=2)
    edges_up = shifted(edges[:, :side], "row", -1)
    edges_down = shifted(edges[:, tile:], "row", 1)
    gap = ((0, 0), (0, tile - side), (0, 0))
    add_edges = jnp.concatenate([edges_down, jnp.zeros((2, tile - side, 2 * width), jnp.float32), edges_up], axis=1)
    edges = edges + add_edges
    add_inner = jnp.concatenate([inner_down, jnp.zeros((2, tile - side, tile - side), jnp.float32), inner_up], axis=1)
    inner = grad_mid[:, :, width : tile - width] + add_inner
    folded = jnp.concatenate([edges[:, :, :width], inner, edges[:, :, width:]], axis=2)
    centre = centre_old - object_rate * folded
    left = shifted(centre[:, :, tile - width :], "col", 1)
    right = shifted(centre[:, :, :width], "col", -1)
    probe_now = probe - probe_gain / frames_total * probe_total

    grad_left, grad_mid, grad_right, probe_part = frames(
        info, (left, centre, right), places, probe_now, intensity, mats, full, full, out_cols
    )

    probe_total = probe_sum(probe_part, probe.shape)
    own = jnp.pad(centre[:, width : width + tile], ((0, 0), (width, width), (0, 0)))
    value_mid = own - object_rate * grad_mid
    value_left = -object_rate * grad_left
    value_right = -object_rate * grad_right
    sent = jnp.concatenate([value_left, value_mid[:, :, :half]], axis=2)
    got = shifted(sent, "col", -1)
    wide = jnp.concatenate(
        [
            value_mid[:, :, half : tile - width],
            value_mid[:, :, tile - width :] + got[:, :, :width],
            value_right + got[:, :, width : 2 * width],
            got[:, :, 2 * width :],
        ],
        axis=2,
    )
    got = shifted(wide[:, : width + half], "row", -1)
    moved = jnp.concatenate(
        [
            wide[:, width + half : tile],
            wide[:, tile : tile + width] + got[:, :width],
            wide[:, tile + width :] + got[:, width : 2 * width],
            got[:, 2 * width :],
        ],
        axis=1,
    )
    return (moved, probe_now - probe_gain / frames_total * probe_total)


def solution(mesh):
    in_specs = (
        P(None, "row", "col"),
        P(),
        P(("row", "col"), None, None),
        P(("row", "col"), None),
        P(("row", "col")),
    )
    out_specs = (P(None, "row", "col"), P())
    return jax.shard_map(
        on_device, mesh=mesh, in_specs=in_specs, out_specs=out_specs, check_vma=False
    )
```

```python
import math

import jax
import jax.numpy as jnp
import numpy as np
from jax import lax
from jax.experimental import pallas as pl
from jax.experimental.pallas import tpu as pltpu
from jax.sharding import PartitionSpec as P

ITERS = 2


object_rate = 0.02
probe_gain = 4.0
LANES = 128
SUBLANES = 8
GROUPS = (4, 2, 1)


def tables(frame_side):
    indices = np.arange(frame_side)
    angle = (indices[:, None] * indices[None, :] % frame_side) * (2.0 * math.pi / frame_side)
    scale = 1.0 / math.sqrt(frame_side)
    real_part = (np.cos(angle) * scale).astype(np.float32).astype(jnp.bfloat16)
    imag_part = (-np.sin(angle) * scale).astype(np.float32).astype(jnp.bfloat16)
    right_mat = np.block([[real_part, imag_part], [-imag_part, real_part]])
    left_mat = np.block([[real_part, -imag_part], [imag_part, real_part]])
    return (jnp.asarray(right_mat), jnp.asarray(left_mat))


def frames_kernel(places, cuts, final, side, info, *refs):
    count, out_count = len(places), len(cuts)
    pieces = refs[:count]
    probe_far, intens, right_far, left_far = refs[count : count + 4]
    outs = refs[count + 4 : count + 4 + out_count]
    probe_grad, region, grad, held, levels, probe, right_mat, left_mat, chosen, in_sems, level_sems, out_sems = refs[
        count + 4 + out_count :
    ]
    arriving = []
    for piece, parts in zip(pieces, places):
        for (row_from, col_from), (row_at, col_at), (rows, cols) in parts:
            arriving.append(
                pltpu.make_async_copy(
                    piece.at[:, row_from : row_from + rows, col_from : col_from + cols],
                    region.at[:, row_at : row_at + rows, col_at : col_at + cols],
                    in_sems.at[len(arriving)],
                )
            )
    for source, target in ((probe_far, probe), (right_far, right_mat), (left_far, left_mat)):
        arriving.append(pltpu.make_async_copy(source, target, in_sems.at[len(arriving)]))
    for copy in arriving:
        copy.start()

    def level_copy(slot):
        return pltpu.make_async_copy(intens.at[slot], levels.at[slot], level_sems.at[slot])

    def pick(slot, found):
        @pl.when(info[slot, 2] != 0)
        def _():
            chosen[found] = slot
            level_copy(slot).start()

        return found + jnp.where(info[slot, 2] != 0, 1, 0)

    total = lax.fori_loop(0, info.shape[0], pick, jnp.int32(0))
    grad[...] = jnp.zeros_like(grad)
    probe_grad[...] = jnp.zeros_like(probe_grad)
    for copy in arriving:
        copy.wait()
    lane = lax.broadcasted_iota(jnp.int32, (side + SUBLANES, LANES), 1)
    line = lax.broadcasted_iota(jnp.int32, (1, SUBLANES, LANES), 1)

    tiles = side // SUBLANES

    def one_group(slots):
        places_of = []
        for lot, slot in enumerate(slots):
            row_at = info[slot, 0]
            col_at = info[slot, 1]
            col_base = pl.multiple_of(col_at // LANES * LANES, LANES)
            row_base = pl.multiple_of(row_at // SUBLANES * SUBLANES, SUBLANES)
            col_shift = col_at - col_base
            row_shift = row_at - row_base
            places_of.append((row_base, col_base, row_shift, col_shift))

        def window(lot, part):
            row_base, col_base, row_shift, col_shift = places_of[lot]
            col_back = jnp.where(col_shift == 0, 0, LANES - col_shift)
            row_back = jnp.where(row_shift == 0, 0, SUBLANES - row_shift)
            inside = lane < LANES - col_shift
            inside_row = line < SUBLANES - row_shift
            rows = pl.ds(row_base, side + SUBLANES)
            turned = [
                pltpu.roll(region[part, rows, pl.ds(pl.multiple_of(col_base + LANES * k, LANES), LANES)], col_back, 1)
                for k in range(3)
            ]
            for k in range(2):
                piece = jnp.where(inside, turned[k], turned[k + 1]).reshape(tiles + 1, SUBLANES, LANES)
                piece = pltpu.roll(piece, row_back, 1)
                piece = jnp.where(inside_row, piece[:tiles], piece[1:]).reshape(side, LANES)
                held[lot, part, :, k * LANES : (k + 1) * LANES] = piece

        def spread(lot, part, value):
            row_base, col_base, row_shift, col_shift = places_of[lot]
            outside = lane >= col_shift
            outside_row = line >= row_shift
            rows = pl.ds(row_base, side + SUBLANES)
            nothing = jnp.zeros((1, SUBLANES, LANES), jnp.float32)
            turned = []
            for k in range(2):
                piece = value[:, k * LANES : (k + 1) * LANES].reshape(tiles, SUBLANES, LANES)
                piece = pltpu.roll(piece, row_shift, 1)
                piece = jnp.where(
                    outside_row,
                    jnp.concatenate([piece, nothing], axis=0),
                    jnp.concatenate([nothing, piece], axis=0),
                ).reshape(side + SUBLANES, LANES)
                turned.append(pltpu.roll(piece, col_shift, 1))
            first, second = turned
            grad[part, rows, pl.ds(col_base, LANES)] += jnp.where(outside, first, 0.0)
            grad[part, rows, pl.ds(pl.multiple_of(col_base + LANES, LANES), LANES)] += jnp.where(outside, second, first)
            grad[part, rows, pl.ds(pl.multiple_of(col_base + 2 * LANES, LANES), LANES)] += jnp.where(outside, 0.0, second)

        lots = range(len(slots))

        def exit_wave(lot):
            window(lot, 0)
            window(lot, 1)
            win_re, win_im = held[lot, 0], held[lot, 1]
            pr_re, pr_im = probe[0], probe[1]
            exit_re = pr_re * win_re - pr_im * win_im
            exit_im = pr_re * win_im + pr_im * win_re
            return jnp.concatenate([exit_re, exit_im], axis=1).astype(jnp.bfloat16)

        def to_wave(flat):
            wave = jnp.dot(flat, right_mat[...], preferred_element_type=jnp.float32).astype(jnp.bfloat16)
            return jnp.concatenate([wave[:, :side], wave[:, side:]], axis=0)

        def to_far(stacked):
            return jnp.dot(left_mat[...], stacked, preferred_element_type=jnp.float32)

        def to_weighted(far, slot):
            far_re, far_im = far[:side], far[side:]
            mismatch = far_re * far_re + far_im * far_im - levels[slot]
            return jnp.concatenate([mismatch * far_re, mismatch * far_im], axis=0).astype(jnp.bfloat16)

        def to_returned(weighted):
            returned = jnp.dot(right_mat[...], weighted, preferred_element_type=jnp.float32).astype(jnp.bfloat16)
            return jnp.concatenate([returned[:side], returned[side:]], axis=1)

        def to_gradient(flat_back):
            return jnp.dot(flat_back, left_mat[...], preferred_element_type=jnp.float32)

        def add(lot, gradient):
            pr_re, pr_im = probe[0], probe[1]
            gr_re, gr_im = gradient[:, :side], gradient[:, side:]
            win_re, win_im = held[lot, 0], held[lot, 1]
            probe_grad[0] += win_re * gr_re + win_im * gr_im
            probe_grad[1] += win_re * gr_im - win_im * gr_re
            spread(lot, 0, pr_re * gr_re + pr_im * gr_im)
            spread(lot, 1, pr_re * gr_im - pr_im * gr_re)

        for slot in slots:
            level_copy(slot).wait()
        waves = [to_wave(exit_wave(lot)) for lot in lots]
        fars = [to_far(wave) for wave in waves]
        weights = [to_weighted(fars[lot], slots[lot]) for lot in lots]
        returns = [to_returned(weighted) for weighted in weights]
        grads = [to_gradient(returned) for returned in returns]
        for lot in lots:
            add(lot, grads[lot])

    done = jnp.int32(0)
    for size in GROUPS:

        def one_step(at, carried, size=size, start=done):
            one_group([chosen[start + size * at + lot] for lot in range(size)])
            return carried

        steps = (total - done) // size
        lax.fori_loop(0, steps, one_step, 0)
        done = done + steps * size
    full = region.shape[1]
    width = side // 2
    if final:
        own = slice(width, full - width)
        for rows, cols in ((slice(0, width), slice(0, full)), (slice(full - width, full), slice(0, full)),
                           (own, slice(0, width)), (own, slice(full - width, full))):
            grad[:, rows, cols] = -object_rate * grad[:, rows, cols]
        grad[:, own, own] = region[:, own, own] - object_rate * grad[:, own, own]
    leaving = []
    for out, parts in zip(outs, cuts):
        for (row_from, col_from), (row_at, col_at), (rows, cols) in parts:
            leaving.append(
                pltpu.make_async_copy(
                    grad.at[:, row_from : row_from + rows, col_from : col_from + cols],
                    out.at[:, row_at : row_at + rows, col_at : col_at + cols],
                    out_sems.at[len(leaving)],
                )
            )
    for copy in leaving:
        copy.start()
    for copy in leaving:
        copy.wait()


def frames(info, placed, probe, intensity, mats, full, cuts, final):
    side = probe.shape[-1]
    vmem = pl.BlockSpec(memory_space=pltpu.VMEM)
    smem = pl.BlockSpec(memory_space=pltpu.SMEM)
    anywhere = pl.BlockSpec(memory_space=pl.ANY)
    far = pl.BlockSpec(memory_space=pltpu.HBM)
    pieces = [piece for piece, parts in placed]
    places = [parts for piece, parts in placed]
    out_shapes = []
    for parts in cuts:
        rows = max(row_at + rows for _, (row_at, _), (rows, _) in parts)
        cols = max(col_at + cols for _, (_, col_at), (_, cols) in parts)
        out_shapes.append(jax.ShapeDtypeStruct((2, rows, cols), jnp.float32))
    out_shapes.append(jax.ShapeDtypeStruct(probe.shape, jnp.float32))

    def kernel(*refs):
        frames_kernel(places, cuts, final, side, *refs)

    return pl.pallas_call(
        kernel,
        out_shape=out_shapes,
        in_specs=[smem] + [anywhere] * len(pieces) + [far] * 4,
        out_specs=[far] * len(cuts) + [vmem],
        scratch_shapes=[
            pltpu.VMEM((2, full, full), jnp.float32),
            pltpu.VMEM((2, full, full), jnp.float32),
            pltpu.VMEM((GROUPS[0], *probe.shape), jnp.float32),
            pltpu.VMEM(intensity.shape, jnp.float32),
            pltpu.VMEM(probe.shape, jnp.float32),
            pltpu.VMEM(mats[0].shape, mats[0].dtype),
            pltpu.VMEM(mats[1].shape, mats[1].dtype),
            pltpu.SMEM((info.shape[0],), jnp.int32),
            pltpu.SemaphoreType.DMA((sum(len(parts) for parts in places) + 3,)),
            pltpu.SemaphoreType.DMA((info.shape[0],)),
            pltpu.SemaphoreType.DMA((sum(len(parts) for parts in cuts),)),
        ],
        compiler_params=pltpu.CompilerParams(vmem_limit_bytes=60 * 1024 * 1024),
        name="frames",
    )(info, *pieces, probe, intensity, *mats)


def shifted(array, axis, by):
    count = lax.axis_size(axis)
    return lax.ppermute(array, axis, [(i, (i + by) % count) for i in range(count)])


def moved(array, axis, by):
    row_count, col_count = lax.axis_size("row"), lax.axis_size("col")
    sizes = {"x": row_count // 2, "z": 4, "y": col_count // 4, "core": 2}
    pairs = []
    for x in range(sizes["x"]):
        for z in range(sizes["z"]):
            for y in range(sizes["y"]):
                for core in range(sizes["core"]):
                    ends = []
                    for step in (0, by):
                        at = {"x": x, "z": z, "y": y, "core": core}
                        at[axis] = (at[axis] + step) % sizes[axis]
                        row = at["x"] * 2 + at["z"] % 2
                        col = (at["z"] // 2) * (col_count // 2) + at["y"] * 2 + at["core"]
                        ends.append(row * col_count + col)
                    pairs.append(tuple(ends))
    return lax.ppermute(array, ("row", "col"), pairs)


def core_and_y():
    col = lax.axis_index("col")
    return (col % 2, col // 2 % (lax.axis_size("col") // 4), lax.axis_size("col") // 4)


def core_share(part):
    core, _, _ = core_and_y()
    halves = part.reshape(2, -1, part.shape[-1])
    mine = lax.dynamic_index_in_dim(halves, core, 0, False)
    other = lax.dynamic_index_in_dim(halves, 1 - core, 0, False)
    return mine + moved(other, "core", 1)


def y_share(half):
    _, y, y_count = core_and_y()
    quarters = half.reshape(y_count, -1, half.shape[-1])
    total = lax.dynamic_index_in_dim(quarters, y, 0, False)
    arrived = [
        moved(lax.dynamic_index_in_dim(quarters, (y + by) % y_count, 0, False), "y", by) for by in range(1, y_count)
    ]
    for value in arrived:
        total = total + value
    return total


def sum_along(total, axis, count):
    for value in [moved(total, axis, by) for by in range(1, count)]:
        total = total + value
    return total


def y_gathered(total):
    _, y, y_count = core_and_y()
    gathered = [total] + [moved(total, "y", by) for by in range(1, y_count)]
    half = jnp.zeros((y_count, *total.shape), jnp.float32)
    for by, value in enumerate(gathered):
        half = lax.dynamic_update_index_in_dim(half, value, (y - by) % y_count, 0)
    return half


def both_halves(half, shape):
    core, _, _ = core_and_y()
    other = moved(half, "core", 1)
    first = jnp.where(core == 0, half, other)
    second = jnp.where(core == 0, other, half)
    return jnp.concatenate([first, second], axis=0).reshape(shape)


def on_device(object_field, probe, intensity, centers, picked):
    tile = object_field.shape[1]
    side = probe.shape[-1]
    width = side // 2
    half = tile // 2
    full = tile + side
    rows_all = tile * lax.axis_size("row")
    cols_all = tile * lax.axis_size("col")
    frames_total = intensity.shape[0] * lax.axis_size("row") * lax.axis_size("col")
    mats = tables(side)
    local_row = (centers[:, 0] - lax.axis_index("row") * tile) % rows_all
    local_col = (centers[:, 1] - lax.axis_index("col") * tile) % cols_all
    info = jnp.stack([local_row, local_col, picked], axis=1)
    low, high, last = width, tile - width, full - width

    def whole(row, col, rows, cols):
        return [((0, 0), (row, col), (rows, cols))]

    def cut(row, col, rows, cols):
        return [((row, col), (0, 0), (rows, cols))]

    def outer(rows):
        return jnp.concatenate([rows[:, :, :width], rows[:, :, high:]], axis=2)

    below_outer = shifted(outer(object_field[:, :width]), "row", -1)
    above_outer = shifted(outer(object_field[:, high:]), "row", 1)
    below_inner = shifted(object_field[:, :width, low:high], "row", -1)
    above_inner = shifted(object_field[:, high:, low:high], "row", 1)
    at_left = shifted(object_field[:, :, high:], "col", 1)
    at_right = shifted(object_field[:, :, :width], "col", -1)
    ends_left = shifted(jnp.concatenate([above_outer[:, :, width:], below_outer[:, :, width:]], axis=1), "col", 1)
    ends_right = shifted(jnp.concatenate([above_outer[:, :, :width], below_outer[:, :, :width]], axis=1), "col", -1)

    def two_columns(row):
        return [((0, 0), (row, width), (width, width)), ((0, width), (row, tile), (width, width))]

    placed = [
        (above_outer, two_columns(0)),
        (above_inner, whole(0, side, width, side)),
        (object_field, whole(width, width, tile, tile)),
        (below_outer, two_columns(last)),
        (below_inner, whole(last, side, width, side)),
        (at_left, whole(width, 0, tile, width)),
        (at_right, whole(width, last, tile, width)),
        (ends_left, [((0, 0), (0, 0), (width, width)), ((width, 0), (last, 0), (width, width))]),
        (ends_right, [((0, 0), (0, last), (width, width)), ((width, 0), (last, last), (width, width))]),
    ]
    both_edges = [((0, width), (0, 0), (full, width)), ((0, tile), (0, width), (full, width))]
    cuts = [
        cut(0, 0, full, width),
        cut(0, last, full, width),
        cut(0, side, side, side),
        cut(tile, side, side, side),
        cut(side, side, side, side),
        both_edges,
    ]
    grad_left, grad_right, inner_top, inner_low, inner_mid, edges, probe_part = frames(
        info, placed, probe, intensity, mats, full, cuts, False
    )

    x_count = lax.axis_size("row") // 2
    inner_up = shifted(inner_top, "row", -1)
    inner_down = shifted(inner_low, "row", 1)
    from_right = shifted(grad_left, "col", -1)
    from_left = shifted(grad_right, "col", 1)
    share = core_share(probe_part)
    share, from_right, from_left, edges, inner_top, inner_low, inner_mid = lax.optimization_barrier(
        (share, from_right, from_left, edges, inner_top, inner_low, inner_mid)
    )
    edges = edges + jnp.concatenate([from_left, from_right], axis=2)
    edges_up = shifted(edges[:, :side], "row", -1)
    edges_down = shifted(edges[:, tile:], "row", 1)
    share = y_share(share)
    share, inner_up, inner_down = lax.optimization_barrier((share, inner_up, inner_down))
    share = sum_along(share, "x", x_count)
    share, edges_up, edges_down = lax.optimization_barrier((share, edges_up, edges_down))
    share = sum_along(share, "z", 4)
    old_edges = jnp.concatenate([above_outer, outer(object_field), below_outer], axis=1)
    new_edges = jnp.concatenate(
        [
            old_edges[:, :side] - object_rate * (edges[:, :side] + edges_down),
            old_edges[:, side:tile] - object_rate * edges[:, side:tile],
            old_edges[:, tile:] - object_rate * (edges[:, tile:] + edges_up),
        ],
        axis=1,
    )
    left = shifted(new_edges[:, :, width:], "col", 1)
    right = shifted(new_edges[:, :, :width], "col", -1)
    share, left, right = lax.optimization_barrier((share, left, right))
    probe_total = both_halves(y_gathered(share), probe.shape)
    old_inner = jnp.concatenate([above_inner, object_field[:, :, low:high], below_inner], axis=1)
    new_inner = jnp.concatenate(
        [
            old_inner[:, :side] - object_rate * (inner_top + inner_down),
            old_inner[:, side:tile] - object_rate * inner_mid,
            old_inner[:, tile:] - object_rate * (inner_low + inner_up),
        ],
        axis=1,
    )
    probe_now = probe - probe_gain / frames_total * probe_total

    placed = [
        (left, whole(0, 0, full, width)),
        (right, whole(0, last, full, width)),
        (new_edges, [((0, 0), (0, width), (full, width)), ((0, width), (0, tile), (full, width))]),
        (new_inner, whole(0, side, full, side)),
    ]
    reach = width + half
    cuts = [
        cut(0, 0, reach, reach),
        cut(reach, 0, full - reach, reach),
        cut(0, reach, reach, width),
        cut(0, tile, reach, 2 * width),
        cut(reach, reach, full - reach, full - reach),
    ]
    out_top, out_rest, here_0, here_1, here_rest, probe_part = frames(
        info, placed, probe_now, intensity, mats, full, cuts, True
    )

    up_0 = shifted(here_0, "row", -1)
    got_top = shifted(out_top, "col", -1)
    share = core_share(probe_part)
    share, got_top, up_0 = lax.optimization_barrier((share, got_top, up_0))
    up_1 = shifted(here_1 + got_top[:, :, : 2 * width], "row", -1)
    share = y_share(share)
    share, out_rest = lax.optimization_barrier((share, out_rest))
    got_rest = shifted(out_rest, "col", -1)
    share = sum_along(share, "x", x_count)
    share, up_1, got_top = lax.optimization_barrier((share, up_1, got_top))
    up_2 = shifted(got_top[:, :, 2 * width :], "row", -1)
    half_sum = y_gathered(sum_along(share, "z", 4))
    half_sum, up_2 = lax.optimization_barrier((half_sum, up_2))
    probe_total = both_halves(half_sum, probe.shape)
    mine = jnp.concatenate(
        [
            here_rest[:, :, :width],
            here_rest[:, :, width : 2 * width] + got_rest[:, :, :width],
            here_rest[:, :, 2 * width :] + got_rest[:, :, width : 2 * width],
            got_rest[:, :, 2 * width :],
        ],
        axis=2,
    )
    got = jnp.concatenate([up_0, up_1, up_2], axis=2)
    moved = jnp.concatenate(
        [mine[:, :width], mine[:, width:] + got[:, : 2 * width], got[:, 2 * width :]], axis=1
    )
    return (moved, probe_now - probe_gain / frames_total * probe_total)


def solution(mesh):
    in_specs = (
        P(None, "row", "col"),
        P(),
        P(("row", "col"), None, None),
        P(("row", "col"), None),
        P(("row", "col")),
    )
    out_specs = (P(None, "row", "col"), P())
    return jax.shard_map(
        on_device, mesh=mesh, in_specs=in_specs, out_specs=out_specs, check_vma=False
    )
```

```python
import math

import jax
import jax.numpy as jnp
import numpy as np
from jax import lax
from jax.experimental import pallas as pl
from jax.experimental.pallas import tpu as pltpu
from jax.sharding import PartitionSpec as P

ITERS = 2


object_rate = 0.02
probe_gain = 4.0
LANES = 128
SUBLANES = 8
GROUP = 4


def tables(frame_side):
    indices = np.arange(frame_side)
    angle = (indices[:, None] * indices[None, :] % frame_side) * (2.0 * math.pi / frame_side)
    scale = 1.0 / math.sqrt(frame_side)
    real_part = (np.cos(angle) * scale).astype(np.float32).astype(jnp.bfloat16)
    imag_part = (-np.sin(angle) * scale).astype(np.float32).astype(jnp.bfloat16)
    right_mat = np.block([[real_part, imag_part], [-imag_part, real_part]])
    left_mat = np.block([[real_part, -imag_part], [imag_part, real_part]])
    return (jnp.asarray(right_mat), jnp.asarray(left_mat))


def frames_kernel(places, cuts, final, side, info, *refs):
    count, out_count = len(places), len(cuts)
    pieces = refs[:count]
    probe_far, intens, right_far, left_far = refs[count : count + 4]
    outs = refs[count + 4 : count + 4 + out_count]
    probe_grad, region, grad, held, levels, probe, right_mat, left_mat, chosen, in_sems, level_sems, out_sems = refs[
        count + 4 + out_count :
    ]
    arriving = []
    for piece, parts in zip(pieces, places):
        for (row_from, col_from), (row_at, col_at), (rows, cols) in parts:
            arriving.append(
                pltpu.make_async_copy(
                    piece.at[:, row_from : row_from + rows, col_from : col_from + cols],
                    region.at[:, row_at : row_at + rows, col_at : col_at + cols],
                    in_sems.at[len(arriving)],
                )
            )
    for source, target in ((probe_far, probe), (right_far, right_mat), (left_far, left_mat)):
        arriving.append(pltpu.make_async_copy(source, target, in_sems.at[len(arriving)]))
    for copy in arriving:
        copy.start()

    def level_copy(slot):
        return pltpu.make_async_copy(intens.at[slot], levels.at[slot], level_sems.at[slot])

    def pick(slot, found):
        @pl.when(info[slot, 2] != 0)
        def _():
            chosen[found] = slot
            level_copy(slot).start()

        return found + jnp.where(info[slot, 2] != 0, 1, 0)

    total = lax.fori_loop(0, info.shape[0], pick, jnp.int32(0))
    grad[...] = jnp.zeros_like(grad)
    probe_grad[...] = jnp.zeros_like(probe_grad)
    for copy in arriving:
        copy.wait()
    lane = lax.broadcasted_iota(jnp.int32, (side + SUBLANES, LANES), 1)
    line = lax.broadcasted_iota(jnp.int32, (1, SUBLANES, LANES), 1)

    tiles = side // SUBLANES

    def one_group(turns):
        slots = [chosen[jnp.minimum(turn, total - 1)] for turn in turns]
        shares = [jnp.where(turn < total, 1.0, 0.0) for turn in turns]
        places_of = []
        for slot in slots:
            row_at = info[slot, 0]
            col_at = info[slot, 1]
            col_base = pl.multiple_of(col_at // LANES * LANES, LANES)
            row_base = pl.multiple_of(row_at // SUBLANES * SUBLANES, SUBLANES)
            col_shift = col_at - col_base
            row_shift = row_at - row_base
            places_of.append((row_base, col_base, row_shift, col_shift))

        def window(lot, part):
            row_base, col_base, row_shift, col_shift = places_of[lot]
            col_back = jnp.where(col_shift == 0, 0, LANES - col_shift)
            row_back = jnp.where(row_shift == 0, 0, SUBLANES - row_shift)
            inside = lane < LANES - col_shift
            inside_row = line < SUBLANES - row_shift
            rows = pl.ds(row_base, side + SUBLANES)
            turned = [
                pltpu.roll(region[part, rows, pl.ds(pl.multiple_of(col_base + LANES * k, LANES), LANES)], col_back, 1)
                for k in range(3)
            ]
            for k in range(2):
                piece = jnp.where(inside, turned[k], turned[k + 1]).reshape(tiles + 1, SUBLANES, LANES)
                piece = pltpu.roll(piece, row_back, 1)
                piece = jnp.where(inside_row, piece[:tiles], piece[1:]).reshape(side, LANES)
                held[lot, part, :, k * LANES : (k + 1) * LANES] = piece

        def spread(lot, part, value):
            row_base, col_base, row_shift, col_shift = places_of[lot]
            outside = lane >= col_shift
            outside_row = line >= row_shift
            rows = pl.ds(row_base, side + SUBLANES)
            nothing = jnp.zeros((1, SUBLANES, LANES), jnp.float32)
            turned = []
            for k in range(2):
                piece = value[:, k * LANES : (k + 1) * LANES].reshape(tiles, SUBLANES, LANES)
                piece = pltpu.roll(piece, row_shift, 1)
                piece = jnp.where(
                    outside_row,
                    jnp.concatenate([piece, nothing], axis=0),
                    jnp.concatenate([nothing, piece], axis=0),
                ).reshape(side + SUBLANES, LANES)
                turned.append(pltpu.roll(piece, col_shift, 1))
            first, second = turned
            grad[part, rows, pl.ds(col_base, LANES)] += jnp.where(outside, first, 0.0)
            grad[part, rows, pl.ds(pl.multiple_of(col_base + LANES, LANES), LANES)] += jnp.where(outside, second, first)
            grad[part, rows, pl.ds(pl.multiple_of(col_base + 2 * LANES, LANES), LANES)] += jnp.where(outside, 0.0, second)

        lots = range(len(slots))

        def exit_wave(lot):
            window(lot, 0)
            window(lot, 1)
            win_re, win_im = held[lot, 0], held[lot, 1]
            pr_re, pr_im = probe[0], probe[1]
            exit_re = pr_re * win_re - pr_im * win_im
            exit_im = pr_re * win_im + pr_im * win_re
            return jnp.concatenate([exit_re, exit_im], axis=1).astype(jnp.bfloat16)

        def to_wave(flat):
            wave = jnp.dot(flat, right_mat[...], preferred_element_type=jnp.float32).astype(jnp.bfloat16)
            return jnp.concatenate([wave[:, :side], wave[:, side:]], axis=0)

        def to_far(stacked):
            return jnp.dot(left_mat[...], stacked, preferred_element_type=jnp.float32)

        def to_weighted(far, lot):
            far_re, far_im = far[:side], far[side:]
            mismatch = (far_re * far_re + far_im * far_im - levels[slots[lot]]) * shares[lot]
            return jnp.concatenate([mismatch * far_re, mismatch * far_im], axis=0).astype(jnp.bfloat16)

        def to_returned(weighted):
            returned = jnp.dot(right_mat[...], weighted, preferred_element_type=jnp.float32).astype(jnp.bfloat16)
            return jnp.concatenate([returned[:side], returned[side:]], axis=1)

        def to_gradient(flat_back):
            return jnp.dot(flat_back, left_mat[...], preferred_element_type=jnp.float32)

        def add(lot, gradient):
            pr_re, pr_im = probe[0], probe[1]
            gr_re, gr_im = gradient[:, :side], gradient[:, side:]
            win_re, win_im = held[lot, 0], held[lot, 1]
            probe_grad[0] += win_re * gr_re + win_im * gr_im
            probe_grad[1] += win_re * gr_im - win_im * gr_re
            spread(lot, 0, pr_re * gr_re + pr_im * gr_im)
            spread(lot, 1, pr_re * gr_im - pr_im * gr_re)

        for turn, slot in zip(turns, slots):

            @pl.when(turn < total)
            def _(slot=slot):
                level_copy(slot).wait()

        waves = [to_wave(exit_wave(lot)) for lot in lots]
        fars = [to_far(wave) for wave in waves]
        weights = [to_weighted(fars[lot], lot) for lot in lots]
        returns = [to_returned(weighted) for weighted in weights]
        grads = [to_gradient(returned) for returned in returns]
        for lot in lots:
            add(lot, grads[lot])

    def one_step(at, carried):
        one_group([GROUP * at + lot for lot in range(GROUP)])
        return carried

    lax.fori_loop(0, (total + GROUP - 1) // GROUP, one_step, 0)
    full = region.shape[1]
    width = side // 2
    if final:
        own = slice(width, full - width)
        for rows, cols in ((slice(0, width), slice(0, full)), (slice(full - width, full), slice(0, full)),
                           (own, slice(0, width)), (own, slice(full - width, full))):
            grad[:, rows, cols] = -object_rate * grad[:, rows, cols]
        grad[:, own, own] = region[:, own, own] - object_rate * grad[:, own, own]
    leaving = []
    for out, parts in zip(outs, cuts):
        for (row_from, col_from), (row_at, col_at), (rows, cols) in parts:
            leaving.append(
                pltpu.make_async_copy(
                    grad.at[:, row_from : row_from + rows, col_from : col_from + cols],
                    out.at[:, row_at : row_at + rows, col_at : col_at + cols],
                    out_sems.at[len(leaving)],
                )
            )
    for copy in leaving:
        copy.start()
    for copy in leaving:
        copy.wait()


def frames(info, placed, probe, intensity, mats, full, cuts, final):
    side = probe.shape[-1]
    vmem = pl.BlockSpec(memory_space=pltpu.VMEM)
    smem = pl.BlockSpec(memory_space=pltpu.SMEM)
    anywhere = pl.BlockSpec(memory_space=pl.ANY)
    far = pl.BlockSpec(memory_space=pltpu.HBM)
    pieces = [piece for piece, parts in placed]
    places = [parts for piece, parts in placed]
    out_shapes = []
    for parts in cuts:
        rows = max(row_at + rows for _, (row_at, _), (rows, _) in parts)
        cols = max(col_at + cols for _, (_, col_at), (_, cols) in parts)
        out_shapes.append(jax.ShapeDtypeStruct((2, rows, cols), jnp.float32))
    out_shapes.append(jax.ShapeDtypeStruct(probe.shape, jnp.float32))

    def kernel(*refs):
        frames_kernel(places, cuts, final, side, *refs)

    return pl.pallas_call(
        kernel,
        out_shape=out_shapes,
        in_specs=[smem] + [anywhere] * len(pieces) + [far] * 4,
        out_specs=[far] * len(cuts) + [vmem],
        scratch_shapes=[
            pltpu.VMEM((2, full, full), jnp.float32),
            pltpu.VMEM((2, full, full), jnp.float32),
            pltpu.VMEM((GROUP, *probe.shape), jnp.float32),
            pltpu.VMEM(intensity.shape, jnp.float32),
            pltpu.VMEM(probe.shape, jnp.float32),
            pltpu.VMEM(mats[0].shape, mats[0].dtype),
            pltpu.VMEM(mats[1].shape, mats[1].dtype),
            pltpu.SMEM((info.shape[0],), jnp.int32),
            pltpu.SemaphoreType.DMA((sum(len(parts) for parts in places) + 3,)),
            pltpu.SemaphoreType.DMA((info.shape[0],)),
            pltpu.SemaphoreType.DMA((sum(len(parts) for parts in cuts),)),
        ],
        compiler_params=pltpu.CompilerParams(vmem_limit_bytes=(40 if final else 60) * 1024 * 1024),
        name="frames",
    )(info, *pieces, probe, intensity, *mats)


def shifted(array, axis, by):
    count = lax.axis_size(axis)
    return lax.ppermute(array, axis, [(i, (i + by) % count) for i in range(count)])


def moved(array, axis, by):
    row_count, col_count = lax.axis_size("row"), lax.axis_size("col")
    sizes = {"x": row_count // 2, "z": 4, "y": col_count // 4, "core": 2}
    pairs = []
    for x in range(sizes["x"]):
        for z in range(sizes["z"]):
            for y in range(sizes["y"]):
                for core in range(sizes["core"]):
                    ends = []
                    for step in (0, by):
                        at = {"x": x, "z": z, "y": y, "core": core}
                        at[axis] = (at[axis] + step) % sizes[axis]
                        row = at["x"] * 2 + at["z"] % 2
                        col = (at["z"] // 2) * (col_count // 2) + at["y"] * 2 + at["core"]
                        ends.append(row * col_count + col)
                    pairs.append(tuple(ends))
    return lax.ppermute(array, ("row", "col"), pairs)


def core_and_y():
    col = lax.axis_index("col")
    return (col % 2, col // 2 % (lax.axis_size("col") // 4), lax.axis_size("col") // 4)


def core_share(part):
    core, _, _ = core_and_y()
    halves = part.reshape(2, -1, part.shape[-1])
    mine = lax.dynamic_index_in_dim(halves, core, 0, False)
    other = lax.dynamic_index_in_dim(halves, 1 - core, 0, False)
    return mine + moved(other, "core", 1)


def y_share(half):
    _, y, y_count = core_and_y()
    quarters = half.reshape(y_count, -1, half.shape[-1])
    total = lax.dynamic_index_in_dim(quarters, y, 0, False)
    arrived = [
        moved(lax.dynamic_index_in_dim(quarters, (y + by) % y_count, 0, False), "y", by) for by in range(1, y_count)
    ]
    for value in arrived:
        total = total + value
    return total


def sum_along(total, axis, count):
    for value in [moved(total, axis, by) for by in range(1, count)]:
        total = total + value
    return total


def y_gathered(total):
    _, y, y_count = core_and_y()
    gathered = [total] + [moved(total, "y", by) for by in range(1, y_count)]
    half = jnp.zeros((y_count, *total.shape), jnp.float32)
    for by, value in enumerate(gathered):
        half = lax.dynamic_update_index_in_dim(half, value, (y - by) % y_count, 0)
    return half


def both_halves(half, shape):
    core, _, _ = core_and_y()
    other = moved(half, "core", 1)
    first = jnp.where(core == 0, half, other)
    second = jnp.where(core == 0, other, half)
    return jnp.concatenate([first, second], axis=0).reshape(shape)


def on_device(object_field, probe, intensity, centers, picked):
    tile = object_field.shape[1]
    side = probe.shape[-1]
    width = side // 2
    half = tile // 2
    full = tile + side
    rows_all = tile * lax.axis_size("row")
    cols_all = tile * lax.axis_size("col")
    frames_total = intensity.shape[0] * lax.axis_size("row") * lax.axis_size("col")
    mats = tables(side)
    local_row = (centers[:, 0] - lax.axis_index("row") * tile) % rows_all
    local_col = (centers[:, 1] - lax.axis_index("col") * tile) % cols_all
    info = jnp.stack([local_row, local_col, picked], axis=1)
    low, high, last = width, tile - width, full - width

    def whole(row, col, rows, cols):
        return [((0, 0), (row, col), (rows, cols))]

    def cut(row, col, rows, cols):
        return [((row, col), (0, 0), (rows, cols))]

    def outer(rows):
        return jnp.concatenate([rows[:, :, :width], rows[:, :, high:]], axis=2)

    below_outer = shifted(outer(object_field[:, :width]), "row", -1)
    above_outer = shifted(outer(object_field[:, high:]), "row", 1)
    below_inner = shifted(object_field[:, :width, low:high], "row", -1)
    above_inner = shifted(object_field[:, high:, low:high], "row", 1)
    at_left = shifted(object_field[:, :, high:], "col", 1)
    at_right = shifted(object_field[:, :, :width], "col", -1)
    ends_left = shifted(jnp.concatenate([above_outer[:, :, width:], below_outer[:, :, width:]], axis=1), "col", 1)
    corners = jnp.concatenate([above_outer[:, :, :width], below_outer[:, :, :width]], axis=1)
    corners, above_inner, below_inner, ends_left = lax.optimization_barrier(
        (corners, above_inner, below_inner, ends_left)
    )
    ends_right = shifted(corners, "col", -1)

    def two_columns(row):
        return [((0, 0), (row, width), (width, width)), ((0, width), (row, tile), (width, width))]

    placed = [
        (above_outer, two_columns(0)),
        (above_inner, whole(0, side, width, side)),
        (object_field, whole(width, width, tile, tile)),
        (below_outer, two_columns(last)),
        (below_inner, whole(last, side, width, side)),
        (at_left, whole(width, 0, tile, width)),
        (at_right, whole(width, last, tile, width)),
        (ends_left, [((0, 0), (0, 0), (width, width)), ((width, 0), (last, 0), (width, width))]),
        (ends_right, [((0, 0), (0, last), (width, width)), ((width, 0), (last, last), (width, width))]),
    ]
    both_edges = [((0, width), (0, 0), (full, width)), ((0, tile), (0, width), (full, width))]
    cuts = [
        cut(0, 0, full, width),
        cut(0, last, full, width),
        cut(0, side, side, side),
        cut(tile, side, side, side),
        cut(side, side, side, side),
        both_edges,
    ]
    grad_left, grad_right, inner_top, inner_low, inner_mid, edges, probe_part = frames(
        info, placed, probe, intensity, mats, full, cuts, False
    )

    x_count = lax.axis_size("row") // 2
    inner_up = shifted(inner_top, "row", -1)
    inner_down = shifted(inner_low, "row", 1)
    from_right = shifted(grad_left, "col", -1)
    from_left = shifted(grad_right, "col", 1)
    share = core_share(probe_part)
    share, from_right, from_left, edges, inner_top, inner_low, inner_mid = lax.optimization_barrier(
        (share, from_right, from_left, edges, inner_top, inner_low, inner_mid)
    )
    edges = edges + jnp.concatenate([from_left, from_right], axis=2)
    edges_up = shifted(edges[:, :side], "row", -1)
    edges_down = shifted(edges[:, tile:], "row", 1)
    share = y_share(share)
    share, inner_up, inner_down = lax.optimization_barrier((share, inner_up, inner_down))
    half_sum = y_gathered(sum_along(sum_along(share, "x", x_count), "z", 4))
    old_edges = jnp.concatenate([above_outer, outer(object_field), below_outer], axis=1)
    new_edges = jnp.concatenate(
        [
            old_edges[:, :side] - object_rate * (edges[:, :side] + edges_down),
            old_edges[:, side:tile] - object_rate * edges[:, side:tile],
            old_edges[:, tile:] - object_rate * (edges[:, tile:] + edges_up),
        ],
        axis=1,
    )
    left = shifted(new_edges[:, :, width:], "col", 1)
    right = shifted(new_edges[:, :, :width], "col", -1)
    half_sum, left, right = lax.optimization_barrier((half_sum, left, right))
    probe_total = both_halves(half_sum, probe.shape)
    old_inner = jnp.concatenate([above_inner, object_field[:, :, low:high], below_inner], axis=1)
    new_inner = jnp.concatenate(
        [
            old_inner[:, :side] - object_rate * (inner_top + inner_down),
            old_inner[:, side:tile] - object_rate * inner_mid,
            old_inner[:, tile:] - object_rate * (inner_low + inner_up),
        ],
        axis=1,
    )
    probe_now = probe - probe_gain / frames_total * probe_total

    placed = [
        (left, whole(0, 0, full, width)),
        (right, whole(0, last, full, width)),
        (new_edges, [((0, 0), (0, width), (full, width)), ((0, width), (0, tile), (full, width))]),
        (new_inner, whole(0, side, full, side)),
    ]
    reach = width + half
    cuts = [
        cut(0, 0, reach, reach),
        cut(reach, 0, full - reach, reach),
        cut(0, reach, reach, width),
        cut(0, tile, reach, 2 * width),
        cut(reach, reach, full - reach, full - reach),
    ]
    out_top, out_rest, here_0, here_1, here_rest, probe_part = frames(
        info, placed, probe_now, intensity, mats, full, cuts, True
    )

    up_0 = shifted(here_0, "row", -1)
    got_top = shifted(out_top, "col", -1)
    share = core_share(probe_part)
    share, got_top, up_0 = lax.optimization_barrier((share, got_top, up_0))
    up_1 = shifted(here_1[:, :, :width] + got_top[:, :, :width], "row", -1)
    up_2 = shifted(here_1[:, :, width:] + got_top[:, :, width : 2 * width], "row", -1)
    up_3 = shifted(got_top[:, :, 2 * width :], "row", -1)
    share = y_share(share)
    share, out_rest, up_1 = lax.optimization_barrier((share, out_rest, up_1))
    got_rest = shifted(out_rest, "col", -1)
    share = sum_along(share, "x", x_count)
    share, up_2, got_rest = lax.optimization_barrier((share, up_2, got_rest))
    half_sum = y_gathered(sum_along(share, "z", 4))
    half_sum, up_3 = lax.optimization_barrier((half_sum, up_3))
    probe_total = both_halves(half_sum, probe.shape)
    mine = jnp.concatenate(
        [
            here_rest[:, :, :width],
            here_rest[:, :, width : 2 * width] + got_rest[:, :, :width],
            here_rest[:, :, 2 * width :] + got_rest[:, :, width : 2 * width],
            got_rest[:, :, 2 * width :],
        ],
        axis=2,
    )
    got = jnp.concatenate([up_0, up_1, up_2, up_3], axis=2)
    moved = jnp.concatenate(
        [mine[:, :width], mine[:, width:] + got[:, : 2 * width], got[:, 2 * width :]], axis=1
    )
    return (moved, probe_now - probe_gain / frames_total * probe_total)


def solution(mesh):
    in_specs = (
        P(None, "row", "col"),
        P(),
        P(("row", "col"), None, None),
        P(("row", "col"), None),
        P(("row", "col")),
    )
    out_specs = (P(None, "row", "col"), P())
    return jax.shard_map(
        on_device, mesh=mesh, in_specs=in_specs, out_specs=out_specs, check_vma=False
    )
```

```python
import math

import jax
import jax.numpy as jnp
import numpy as np
from jax import lax
from jax.experimental import pallas as pl
from jax.experimental.pallas import tpu as pltpu
from jax.sharding import PartitionSpec as P

ITERS = 2


object_rate = 0.02
probe_gain = 4.0
LANES = 128
SUBLANES = 8
GROUP = 4


def tables(frame_side):
    indices = np.arange(frame_side)
    angle = (indices[:, None] * indices[None, :] % frame_side) * (2.0 * math.pi / frame_side)
    scale = 1.0 / math.sqrt(frame_side)
    real_part = (np.cos(angle) * scale).astype(np.float32).astype(jnp.bfloat16)
    imag_part = (-np.sin(angle) * scale).astype(np.float32).astype(jnp.bfloat16)
    right_mat = np.block([[real_part, imag_part], [-imag_part, real_part]])
    left_mat = np.block([[real_part, -imag_part], [imag_part, real_part]])
    return (jnp.asarray(right_mat), jnp.asarray(left_mat))


def frames_kernel(places, cuts, final, side, info, *refs):
    count, out_count = len(places), len(cuts)
    pieces = refs[:count]
    probe_far, intens, right_far, left_far = refs[count : count + 4]
    outs = refs[count + 4 : count + 4 + out_count]
    probe_grad, region, grad, held, levels, probe, right_mat, left_mat, chosen, in_sems, level_sems, out_sems = refs[
        count + 4 + out_count :
    ]
    arriving = []
    for piece, parts in zip(pieces, places):
        for (row_from, col_from), (row_at, col_at), (rows, cols) in parts:
            arriving.append(
                pltpu.make_async_copy(
                    piece.at[:, row_from : row_from + rows, col_from : col_from + cols],
                    region.at[:, row_at : row_at + rows, col_at : col_at + cols],
                    in_sems.at[len(arriving)],
                )
            )
    for source, target in ((probe_far, probe), (right_far, right_mat), (left_far, left_mat)):
        arriving.append(pltpu.make_async_copy(source, target, in_sems.at[len(arriving)]))
    for copy in arriving:
        copy.start()

    def level_copy(slot):
        return pltpu.make_async_copy(intens.at[slot], levels.at[slot], level_sems.at[slot])

    def pick(slot, found):
        @pl.when(info[slot, 2] != 0)
        def _():
            chosen[found] = slot
            level_copy(slot).start()

        return found + jnp.where(info[slot, 2] != 0, 1, 0)

    total = lax.fori_loop(0, info.shape[0], pick, jnp.int32(0))
    grad[...] = jnp.zeros_like(grad)
    probe_grad[...] = jnp.zeros_like(probe_grad)
    for copy in arriving:
        copy.wait()
    lane = lax.broadcasted_iota(jnp.int32, (side + SUBLANES, LANES), 1)
    line = lax.broadcasted_iota(jnp.int32, (1, SUBLANES, LANES), 1)

    tiles = side // SUBLANES

    def one_group(turns):
        slots = [chosen[jnp.minimum(turn, total - 1)] for turn in turns]
        shares = [jnp.where(turn < total, 1.0, 0.0) for turn in turns]
        places_of = []
        for slot in slots:
            row_at = info[slot, 0]
            col_at = info[slot, 1]
            col_base = pl.multiple_of(col_at // LANES * LANES, LANES)
            row_base = pl.multiple_of(row_at // SUBLANES * SUBLANES, SUBLANES)
            col_shift = col_at - col_base
            row_shift = row_at - row_base
            places_of.append((row_base, col_base, row_shift, col_shift))

        def window(lot, part):
            row_base, col_base, row_shift, col_shift = places_of[lot]
            col_back = jnp.where(col_shift == 0, 0, LANES - col_shift)
            row_back = jnp.where(row_shift == 0, 0, SUBLANES - row_shift)
            inside = lane < LANES - col_shift
            inside_row = line < SUBLANES - row_shift
            rows = pl.ds(row_base, side + SUBLANES)
            turned = [
                pltpu.roll(region[part, rows, pl.ds(pl.multiple_of(col_base + LANES * k, LANES), LANES)], col_back, 1)
                for k in range(3)
            ]
            for k in range(2):
                piece = jnp.where(inside, turned[k], turned[k + 1]).reshape(tiles + 1, SUBLANES, LANES)
                piece = pltpu.roll(piece, row_back, 1)
                piece = jnp.where(inside_row, piece[:tiles], piece[1:]).reshape(side, LANES)
                held[lot, part, :, k * LANES : (k + 1) * LANES] = piece

        def spread(lot, part, value):
            row_base, col_base, row_shift, col_shift = places_of[lot]
            outside = lane >= col_shift
            outside_row = line >= row_shift
            rows = pl.ds(row_base, side + SUBLANES)
            nothing = jnp.zeros((1, SUBLANES, LANES), jnp.float32)
            turned = []
            for k in range(2):
                piece = value[:, k * LANES : (k + 1) * LANES].reshape(tiles, SUBLANES, LANES)
                piece = pltpu.roll(piece, row_shift, 1)
                piece = jnp.where(
                    outside_row,
                    jnp.concatenate([piece, nothing], axis=0),
                    jnp.concatenate([nothing, piece], axis=0),
                ).reshape(side + SUBLANES, LANES)
                turned.append(pltpu.roll(piece, col_shift, 1))
            first, second = turned
            grad[part, rows, pl.ds(col_base, LANES)] += jnp.where(outside, first, 0.0)
            grad[part, rows, pl.ds(pl.multiple_of(col_base + LANES, LANES), LANES)] += jnp.where(outside, second, first)
            grad[part, rows, pl.ds(pl.multiple_of(col_base + 2 * LANES, LANES), LANES)] += jnp.where(outside, 0.0, second)

        lots = range(len(slots))

        def exit_wave(lot):
            window(lot, 0)
            window(lot, 1)
            win_re, win_im = held[lot, 0], held[lot, 1]
            pr_re, pr_im = probe[0], probe[1]
            exit_re = pr_re * win_re - pr_im * win_im
            exit_im = pr_re * win_im + pr_im * win_re
            return jnp.concatenate([exit_re, exit_im], axis=1).astype(jnp.bfloat16)

        def to_wave(flat):
            wave = jnp.dot(flat, right_mat[...], preferred_element_type=jnp.float32).astype(jnp.bfloat16)
            return jnp.concatenate([wave[:, :side], wave[:, side:]], axis=0)

        def to_far(stacked):
            return jnp.dot(left_mat[...], stacked, preferred_element_type=jnp.float32)

        def to_weighted(far, lot):
            far_re, far_im = far[:side], far[side:]
            mismatch = (far_re * far_re + far_im * far_im - levels[slots[lot]]) * shares[lot]
            return jnp.concatenate([mismatch * far_re, mismatch * far_im], axis=0).astype(jnp.bfloat16)

        def to_returned(weighted):
            returned = jnp.dot(right_mat[...], weighted, preferred_element_type=jnp.float32).astype(jnp.bfloat16)
            return jnp.concatenate([returned[:side], returned[side:]], axis=1)

        def to_gradient(flat_back):
            return jnp.dot(flat_back, left_mat[...], preferred_element_type=jnp.float32)

        def add(lot, gradient):
            pr_re, pr_im = probe[0], probe[1]
            gr_re, gr_im = gradient[:, :side], gradient[:, side:]
            win_re, win_im = held[lot, 0], held[lot, 1]
            probe_grad[0] += win_re * gr_re + win_im * gr_im
            probe_grad[1] += win_re * gr_im - win_im * gr_re
            spread(lot, 0, pr_re * gr_re + pr_im * gr_im)
            spread(lot, 1, pr_re * gr_im - pr_im * gr_re)

        for turn, slot in zip(turns, slots):

            @pl.when(turn < total)
            def _(slot=slot):
                level_copy(slot).wait()

        waves = [to_wave(exit_wave(lot)) for lot in lots]
        fars = [to_far(wave) for wave in waves]
        weights = [to_weighted(fars[lot], lot) for lot in lots]
        returns = [to_returned(weighted) for weighted in weights]
        grads = [to_gradient(returned) for returned in returns]
        for lot in lots:
            add(lot, grads[lot])

    def one_step(at, carried):
        one_group([GROUP * at + lot for lot in range(GROUP)])
        return carried

    lax.fori_loop(0, (total + GROUP - 1) // GROUP, one_step, 0)
    full = region.shape[1]
    width = side // 2
    if final:
        own = slice(width, full - width)
        for rows, cols in ((slice(0, width), slice(0, full)), (slice(full - width, full), slice(0, full)),
                           (own, slice(0, width)), (own, slice(full - width, full))):
            grad[:, rows, cols] = -object_rate * grad[:, rows, cols]
        grad[:, own, own] = region[:, own, own] - object_rate * grad[:, own, own]
    leaving = []
    for out, parts in zip(outs, cuts):
        for (row_from, col_from), (row_at, col_at), (rows, cols) in parts:
            leaving.append(
                pltpu.make_async_copy(
                    grad.at[:, row_from : row_from + rows, col_from : col_from + cols],
                    out.at[:, row_at : row_at + rows, col_at : col_at + cols],
                    out_sems.at[len(leaving)],
                )
            )
    for copy in leaving:
        copy.start()
    for copy in leaving:
        copy.wait()


def frames(info, placed, probe, intensity, mats, full, cuts, final):
    side = probe.shape[-1]
    vmem = pl.BlockSpec(memory_space=pltpu.VMEM)
    smem = pl.BlockSpec(memory_space=pltpu.SMEM)
    anywhere = pl.BlockSpec(memory_space=pl.ANY)
    far = pl.BlockSpec(memory_space=pltpu.HBM)
    pieces = [piece for piece, parts in placed]
    places = [parts for piece, parts in placed]
    out_shapes = []
    for parts in cuts:
        rows = max(row_at + rows for _, (row_at, _), (rows, _) in parts)
        cols = max(col_at + cols for _, (_, col_at), (_, cols) in parts)
        out_shapes.append(jax.ShapeDtypeStruct((2, rows, cols), jnp.float32))
    out_shapes.append(jax.ShapeDtypeStruct(probe.shape, jnp.float32))

    def kernel(*refs):
        frames_kernel(places, cuts, final, side, *refs)

    return pl.pallas_call(
        kernel,
        out_shape=out_shapes,
        in_specs=[smem] + [anywhere] * len(pieces) + [far] * 4,
        out_specs=[far] * len(cuts) + [vmem],
        scratch_shapes=[
            pltpu.VMEM((2, full, full), jnp.float32),
            pltpu.VMEM((2, full, full), jnp.float32),
            pltpu.VMEM((GROUP, *probe.shape), jnp.float32),
            pltpu.VMEM(intensity.shape, jnp.float32),
            pltpu.VMEM(probe.shape, jnp.float32),
            pltpu.VMEM(mats[0].shape, mats[0].dtype),
            pltpu.VMEM(mats[1].shape, mats[1].dtype),
            pltpu.SMEM((info.shape[0],), jnp.int32),
            pltpu.SemaphoreType.DMA((sum(len(parts) for parts in places) + 3,)),
            pltpu.SemaphoreType.DMA((info.shape[0],)),
            pltpu.SemaphoreType.DMA((sum(len(parts) for parts in cuts),)),
        ],
        compiler_params=pltpu.CompilerParams(vmem_limit_bytes=(40 if final else 60) * 1024 * 1024),
        name="frames",
    )(info, *pieces, probe, intensity, *mats)


def shifted(array, axis, by):
    count = lax.axis_size(axis)
    return lax.ppermute(array, axis, [(i, (i + by) % count) for i in range(count)])


def moved(array, axis, by):
    row_count, col_count = lax.axis_size("row"), lax.axis_size("col")
    sizes = {"x": row_count // 2, "z": 4, "y": col_count // 4, "core": 2}
    pairs = []
    for x in range(sizes["x"]):
        for z in range(sizes["z"]):
            for y in range(sizes["y"]):
                for core in range(sizes["core"]):
                    ends = []
                    for step in (0, by):
                        at = {"x": x, "z": z, "y": y, "core": core}
                        at[axis] = (at[axis] + step) % sizes[axis]
                        row = at["x"] * 2 + at["z"] % 2
                        col = (at["z"] // 2) * (col_count // 2) + at["y"] * 2 + at["core"]
                        ends.append(row * col_count + col)
                    pairs.append(tuple(ends))
    return lax.ppermute(array, ("row", "col"), pairs)


def core_and_x():
    return (lax.axis_index("col") % 2, lax.axis_index("row") // 2, lax.axis_size("row") // 2)


def core_share(part):
    core, _, _ = core_and_x()
    halves = part.reshape(2, -1, part.shape[-1])
    mine = lax.dynamic_index_in_dim(halves, core, 0, False)
    other = lax.dynamic_index_in_dim(halves, 1 - core, 0, False)
    return mine + moved(other, "core", 1)


def x_share(half):
    _, x, x_count = core_and_x()
    parts = half.reshape(x_count, -1, half.shape[-1])
    total = lax.dynamic_index_in_dim(parts, x, 0, False)
    arrived = [
        moved(lax.dynamic_index_in_dim(parts, (x + by) % x_count, 0, False), "x", by) for by in range(1, x_count)
    ]
    for value in arrived:
        total = total + value
    return total


def sum_along(total, axis, count):
    for value in [moved(total, axis, by) for by in range(1, count)]:
        total = total + value
    return total


def x_gathered(total):
    _, x, x_count = core_and_x()
    gathered = [total] + [moved(total, "x", by) for by in range(1, x_count)]
    half = jnp.zeros((x_count, *total.shape), jnp.float32)
    for by, value in enumerate(gathered):
        half = lax.dynamic_update_index_in_dim(half, value, (x - by) % x_count, 0)
    return half


def both_halves(half, shape):
    core, _, _ = core_and_x()
    other = moved(half, "core", 1)
    first = jnp.where(core == 0, half, other)
    second = jnp.where(core == 0, other, half)
    return jnp.concatenate([first, second], axis=0).reshape(shape)


def on_device(object_field, probe, intensity, centers, picked):
    tile = object_field.shape[1]
    side = probe.shape[-1]
    width = side // 2
    half = tile // 2
    full = tile + side
    rows_all = tile * lax.axis_size("row")
    cols_all = tile * lax.axis_size("col")
    frames_total = intensity.shape[0] * lax.axis_size("row") * lax.axis_size("col")
    mats = tables(side)
    local_row = (centers[:, 0] - lax.axis_index("row") * tile) % rows_all
    local_col = (centers[:, 1] - lax.axis_index("col") * tile) % cols_all
    info = jnp.stack([local_row, local_col, picked], axis=1)
    low, high, last = width, tile - width, full - width

    def whole(row, col, rows, cols):
        return [((0, 0), (row, col), (rows, cols))]

    def cut(row, col, rows, cols):
        return [((row, col), (0, 0), (rows, cols))]

    def outer(rows):
        return jnp.concatenate([rows[:, :, :width], rows[:, :, high:]], axis=2)

    below_outer = shifted(outer(object_field[:, :width]), "row", -1)
    above_outer = shifted(outer(object_field[:, high:]), "row", 1)
    below_inner = shifted(object_field[:, :width, low:high], "row", -1)
    above_inner = shifted(object_field[:, high:, low:high], "row", 1)
    at_left = shifted(object_field[:, :, high:], "col", 1)
    at_right = shifted(object_field[:, :, :width], "col", -1)
    ends_left = shifted(jnp.concatenate([above_outer[:, :, width:], below_outer[:, :, width:]], axis=1), "col", 1)
    corners = jnp.concatenate([above_outer[:, :, :width], below_outer[:, :, :width]], axis=1)
    corners, above_inner, below_inner, ends_left = lax.optimization_barrier(
        (corners, above_inner, below_inner, ends_left)
    )
    ends_right = shifted(corners, "col", -1)

    def two_columns(row):
        return [((0, 0), (row, width), (width, width)), ((0, width), (row, tile), (width, width))]

    placed = [
        (above_outer, two_columns(0)),
        (above_inner, whole(0, side, width, side)),
        (object_field, whole(width, width, tile, tile)),
        (below_outer, two_columns(last)),
        (below_inner, whole(last, side, width, side)),
        (at_left, whole(width, 0, tile, width)),
        (at_right, whole(width, last, tile, width)),
        (ends_left, [((0, 0), (0, 0), (width, width)), ((width, 0), (last, 0), (width, width))]),
        (ends_right, [((0, 0), (0, last), (width, width)), ((width, 0), (last, last), (width, width))]),
    ]
    both_edges = [((0, width), (0, 0), (full, width)), ((0, tile), (0, width), (full, width))]
    cuts = [
        cut(0, 0, full, width),
        cut(0, last, full, width),
        cut(0, side, side, side),
        cut(tile, side, side, side),
        cut(side, side, side, side),
        both_edges,
    ]
    grad_left, grad_right, inner_top, inner_low, inner_mid, edges, probe_part = frames(
        info, placed, probe, intensity, mats, full, cuts, False
    )

    y_count = lax.axis_size("col") // 4
    inner_up = shifted(inner_top, "row", -1)
    inner_down = shifted(inner_low, "row", 1)
    from_right = shifted(grad_left, "col", -1)
    from_left = shifted(grad_right, "col", 1)
    share = x_share(core_share(probe_part))
    share, from_right, from_left, edges, inner_top, inner_low, inner_mid = lax.optimization_barrier(
        (share, from_right, from_left, edges, inner_top, inner_low, inner_mid)
    )
    edges = edges + jnp.concatenate([from_left, from_right], axis=2)
    edges_up = shifted(edges[:, :side], "row", -1)
    edges_down = shifted(edges[:, tile:], "row", 1)
    share = sum_along(share, "y", y_count)
    share, inner_up, inner_down = lax.optimization_barrier((share, inner_up, inner_down))
    half_sum = x_gathered(sum_along(share, "z", 4))
    old_edges = jnp.concatenate([above_outer, outer(object_field), below_outer], axis=1)
    new_edges = jnp.concatenate(
        [
            old_edges[:, :side] - object_rate * (edges[:, :side] + edges_down),
            old_edges[:, side:tile] - object_rate * edges[:, side:tile],
            old_edges[:, tile:] - object_rate * (edges[:, tile:] + edges_up),
        ],
        axis=1,
    )
    left = shifted(new_edges[:, :, width:], "col", 1)
    right = shifted(new_edges[:, :, :width], "col", -1)
    half_sum, left, right = lax.optimization_barrier((half_sum, left, right))
    probe_total = both_halves(half_sum, probe.shape)
    old_inner = jnp.concatenate([above_inner, object_field[:, :, low:high], below_inner], axis=1)
    new_inner = jnp.concatenate(
        [
            old_inner[:, :side] - object_rate * (inner_top + inner_down),
            old_inner[:, side:tile] - object_rate * inner_mid,
            old_inner[:, tile:] - object_rate * (inner_low + inner_up),
        ],
        axis=1,
    )
    probe_now = probe - probe_gain / frames_total * probe_total

    placed = [
        (left, whole(0, 0, full, width)),
        (right, whole(0, last, full, width)),
        (new_edges, [((0, 0), (0, width), (full, width)), ((0, width), (0, tile), (full, width))]),
        (new_inner, whole(0, side, full, side)),
    ]
    reach = width + half
    cuts = [
        cut(0, 0, reach, reach),
        cut(reach, 0, full - reach, reach),
        cut(0, reach, reach, width),
        cut(0, tile, reach, 2 * width),
        cut(reach, reach, full - reach, full - reach),
    ]
    out_top, out_rest, here_0, here_1, here_rest, probe_part = frames(
        info, placed, probe_now, intensity, mats, full, cuts, True
    )

    up_0 = shifted(here_0, "row", -1)
    got_top = shifted(out_top, "col", -1)
    share = x_share(core_share(probe_part))
    share, got_top, up_0 = lax.optimization_barrier((share, got_top, up_0))
    up_1 = shifted(here_1[:, :, :width] + got_top[:, :, :width], "row", -1)
    up_2 = shifted(here_1[:, :, width:] + got_top[:, :, width : 2 * width], "row", -1)
    up_3 = shifted(got_top[:, :, 2 * width :], "row", -1)
    share = sum_along(share, "y", y_count)
    share, up_1, up_2, out_rest = lax.optimization_barrier((share, up_1, up_2, out_rest))
    got_rest = shifted(out_rest, "col", -1)
    half_sum = x_gathered(sum_along(share, "z", 4))
    half_sum, up_3 = lax.optimization_barrier((half_sum, up_3))
    probe_total = both_halves(half_sum, probe.shape)
    mine = jnp.concatenate(
        [
            here_rest[:, :, :width],
            here_rest[:, :, width : 2 * width] + got_rest[:, :, :width],
            here_rest[:, :, 2 * width :] + got_rest[:, :, width : 2 * width],
            got_rest[:, :, 2 * width :],
        ],
        axis=2,
    )
    got = jnp.concatenate([up_0, up_1, up_2, up_3], axis=2)
    moved = jnp.concatenate(
        [mine[:, :width], mine[:, width:] + got[:, : 2 * width], got[:, 2 * width :]], axis=1
    )
    return (moved, probe_now - probe_gain / frames_total * probe_total)


def solution(mesh):
    in_specs = (
        P(None, "row", "col"),
        P(),
        P(("row", "col"), None, None),
        P(("row", "col"), None),
        P(("row", "col")),
    )
    out_specs = (P(None, "row", "col"), P())
    return jax.shard_map(
        on_device, mesh=mesh, in_specs=in_specs, out_specs=out_specs, check_vma=False
    )
```

```python
import math

import jax
import jax.numpy as jnp
import numpy as np
from jax import lax
from jax.experimental import pallas as pl
from jax.experimental.pallas import tpu as pltpu
from jax.sharding import PartitionSpec as P

ITERS = 2


object_rate = 0.02
probe_gain = 4.0
LANES = 128
SUBLANES = 8
GROUP = 4
STAGGER = 1


def tables(frame_side):
    indices = np.arange(frame_side)
    angle = (indices[:, None] * indices[None, :] % frame_side) * (2.0 * math.pi / frame_side)
    scale = 1.0 / math.sqrt(frame_side)
    real_part = (np.cos(angle) * scale).astype(np.float32).astype(jnp.bfloat16)
    imag_part = (-np.sin(angle) * scale).astype(np.float32).astype(jnp.bfloat16)
    right_mat = np.block([[real_part, imag_part], [-imag_part, real_part]])
    left_mat = np.block([[real_part, -imag_part], [imag_part, real_part]])
    return (jnp.asarray(right_mat), jnp.asarray(left_mat))


def frames_kernel(places, cuts, final, side, info, *refs):
    count, out_count = len(places), len(cuts)
    pieces = refs[:count]
    probe_far, intens, right_far, left_far = refs[count : count + 4]
    outs = refs[count + 4 : count + 4 + out_count]
    probe_grad, region, grad, held, levels, probe, right_mat, left_mat, chosen, in_sems, level_sems, out_sems = refs[
        count + 4 + out_count :
    ]
    arriving = []
    for piece, parts in zip(pieces, places):
        for (row_from, col_from), (row_at, col_at), (rows, cols) in parts:
            arriving.append(
                pltpu.make_async_copy(
                    piece.at[:, row_from : row_from + rows, col_from : col_from + cols],
                    region.at[:, row_at : row_at + rows, col_at : col_at + cols],
                    in_sems.at[len(arriving)],
                )
            )
    for source, target in ((probe_far, probe), (right_far, right_mat), (left_far, left_mat)):
        arriving.append(pltpu.make_async_copy(source, target, in_sems.at[len(arriving)]))
    for copy in arriving:
        copy.start()

    def level_copy(slot):
        return pltpu.make_async_copy(intens.at[slot], levels.at[slot], level_sems.at[slot])

    def pick(slot, found):
        @pl.when(info[slot, 2] != 0)
        def _():
            chosen[found] = slot
            level_copy(slot).start()

        return found + jnp.where(info[slot, 2] != 0, 1, 0)

    total = lax.fori_loop(0, info.shape[0], pick, jnp.int32(0))
    grad[...] = jnp.zeros_like(grad)
    probe_grad[...] = jnp.zeros_like(probe_grad)
    for copy in arriving:
        copy.wait()
    lane = lax.broadcasted_iota(jnp.int32, (side + SUBLANES, LANES), 1)
    line = lax.broadcasted_iota(jnp.int32, (1, SUBLANES, LANES), 1)

    tiles = side // SUBLANES

    def one_group(turns):
        slots = [chosen[jnp.minimum(turn, total - 1)] for turn in turns]
        shares = [jnp.where(turn < total, 1.0, 0.0) for turn in turns]
        places_of = []
        for slot in slots:
            row_at = info[slot, 0]
            col_at = info[slot, 1]
            col_base = pl.multiple_of(col_at // LANES * LANES, LANES)
            row_base = pl.multiple_of(row_at // SUBLANES * SUBLANES, SUBLANES)
            col_shift = col_at - col_base
            row_shift = row_at - row_base
            places_of.append((row_base, col_base, row_shift, col_shift))

        def window(lot, part):
            row_base, col_base, row_shift, col_shift = places_of[lot]
            col_back = jnp.where(col_shift == 0, 0, LANES - col_shift)
            row_back = jnp.where(row_shift == 0, 0, SUBLANES - row_shift)
            inside = lane < LANES - col_shift
            inside_row = line < SUBLANES - row_shift
            rows = pl.ds(row_base, side + SUBLANES)
            turned = [
                pltpu.roll(region[part, rows, pl.ds(pl.multiple_of(col_base + LANES * k, LANES), LANES)], col_back, 1)
                for k in range(3)
            ]
            for k in range(2):
                piece = jnp.where(inside, turned[k], turned[k + 1]).reshape(tiles + 1, SUBLANES, LANES)
                piece = pltpu.roll(piece, row_back, 1)
                piece = jnp.where(inside_row, piece[:tiles], piece[1:]).reshape(side, LANES)
                held[lot, part, :, k * LANES : (k + 1) * LANES] = piece

        def spread(lot, part, value):
            row_base, col_base, row_shift, col_shift = places_of[lot]
            outside = lane >= col_shift
            outside_row = line >= row_shift
            rows = pl.ds(row_base, side + SUBLANES)
            nothing = jnp.zeros((1, SUBLANES, LANES), jnp.float32)
            turned = []
            for k in range(2):
                piece = value[:, k * LANES : (k + 1) * LANES].reshape(tiles, SUBLANES, LANES)
                piece = pltpu.roll(piece, row_shift, 1)
                piece = jnp.where(
                    outside_row,
                    jnp.concatenate([piece, nothing], axis=0),
                    jnp.concatenate([nothing, piece], axis=0),
                ).reshape(side + SUBLANES, LANES)
                turned.append(pltpu.roll(piece, col_shift, 1))
            first, second = turned
            grad[part, rows, pl.ds(col_base, LANES)] += jnp.where(outside, first, 0.0)
            grad[part, rows, pl.ds(pl.multiple_of(col_base + LANES, LANES), LANES)] += jnp.where(outside, second, first)
            grad[part, rows, pl.ds(pl.multiple_of(col_base + 2 * LANES, LANES), LANES)] += jnp.where(outside, 0.0, second)

        lots = range(len(slots))

        def exit_wave(lot):
            window(lot, 0)
            window(lot, 1)
            win_re, win_im = held[lot, 0], held[lot, 1]
            pr_re, pr_im = probe[0], probe[1]
            exit_re = pr_re * win_re - pr_im * win_im
            exit_im = pr_re * win_im + pr_im * win_re
            return jnp.concatenate([exit_re, exit_im], axis=1).astype(jnp.bfloat16)

        def to_wave(flat):
            wave = jnp.dot(flat, right_mat[...], preferred_element_type=jnp.float32).astype(jnp.bfloat16)
            return jnp.concatenate([wave[:, :side], wave[:, side:]], axis=0)

        def to_far(stacked):
            return jnp.dot(left_mat[...], stacked, preferred_element_type=jnp.float32)

        def to_weighted(far, lot):
            far_re, far_im = far[:side], far[side:]
            mismatch = (far_re * far_re + far_im * far_im - levels[slots[lot]]) * shares[lot]
            return jnp.concatenate([mismatch * far_re, mismatch * far_im], axis=0).astype(jnp.bfloat16)

        def to_returned(weighted):
            returned = jnp.dot(right_mat[...], weighted, preferred_element_type=jnp.float32).astype(jnp.bfloat16)
            return jnp.concatenate([returned[:side], returned[side:]], axis=1)

        def to_gradient(flat_back):
            return jnp.dot(flat_back, left_mat[...], preferred_element_type=jnp.float32)

        def add(lot, gradient):
            pr_re, pr_im = probe[0], probe[1]
            gr_re, gr_im = gradient[:, :side], gradient[:, side:]
            win_re, win_im = held[lot, 0], held[lot, 1]
            probe_grad[0] += win_re * gr_re + win_im * gr_im
            probe_grad[1] += win_re * gr_im - win_im * gr_re
            spread(lot, 0, pr_re * gr_re + pr_im * gr_im)
            spread(lot, 1, pr_re * gr_im - pr_im * gr_re)

        for turn, slot in zip(turns, slots):

            @pl.when(turn < total)
            def _(slot=slot):
                level_copy(slot).wait()

        stages = (
            lambda lot, value: exit_wave(lot),
            lambda lot, value: to_wave(value),
            lambda lot, value: to_far(value),
            lambda lot, value: to_weighted(value, lot),
            lambda lot, value: to_returned(value),
            lambda lot, value: to_gradient(value),
            add,
        )
        values = [None] * len(slots)
        for tick in range(len(stages) + STAGGER * (len(slots) - 1)):
            for lot in lots:
                stage = tick - STAGGER * lot
                if 0 <= stage < len(stages):
                    values[lot] = stages[stage](lot, values[lot])

    def one_step(at, carried):
        one_group([GROUP * at + lot for lot in range(GROUP)])
        return carried

    lax.fori_loop(0, (total + GROUP - 1) // GROUP, one_step, 0)
    full = region.shape[1]
    width = side // 2
    if final:
        own = slice(width, full - width)
        for rows, cols in ((slice(0, width), slice(0, full)), (slice(full - width, full), slice(0, full)),
                           (own, slice(0, width)), (own, slice(full - width, full))):
            grad[:, rows, cols] = -object_rate * grad[:, rows, cols]
        grad[:, own, own] = region[:, own, own] - object_rate * grad[:, own, own]
    leaving = []
    for out, parts in zip(outs, cuts):
        for (row_from, col_from), (row_at, col_at), (rows, cols) in parts:
            leaving.append(
                pltpu.make_async_copy(
                    grad.at[:, row_from : row_from + rows, col_from : col_from + cols],
                    out.at[:, row_at : row_at + rows, col_at : col_at + cols],
                    out_sems.at[len(leaving)],
                )
            )
    for copy in leaving:
        copy.start()
    for copy in leaving:
        copy.wait()


def frames(info, placed, probe, intensity, mats, full, cuts, final):
    side = probe.shape[-1]
    vmem = pl.BlockSpec(memory_space=pltpu.VMEM)
    smem = pl.BlockSpec(memory_space=pltpu.SMEM)
    anywhere = pl.BlockSpec(memory_space=pl.ANY)
    far = pl.BlockSpec(memory_space=pltpu.HBM)
    pieces = [piece for piece, parts in placed]
    places = [parts for piece, parts in placed]
    out_shapes = []
    for parts in cuts:
        rows = max(row_at + rows for _, (row_at, _), (rows, _) in parts)
        cols = max(col_at + cols for _, (_, col_at), (_, cols) in parts)
        out_shapes.append(jax.ShapeDtypeStruct((2, rows, cols), jnp.float32))
    out_shapes.append(jax.ShapeDtypeStruct(probe.shape, jnp.float32))

    def kernel(*refs):
        frames_kernel(places, cuts, final, side, *refs)

    return pl.pallas_call(
        kernel,
        out_shape=out_shapes,
        in_specs=[smem] + [anywhere] * len(pieces) + [far] * 4,
        out_specs=[far] * len(cuts) + [vmem],
        scratch_shapes=[
            pltpu.VMEM((2, full, full), jnp.float32),
            pltpu.VMEM((2, full, full), jnp.float32),
            pltpu.VMEM((GROUP, *probe.shape), jnp.float32),
            pltpu.VMEM(intensity.shape, jnp.float32),
            pltpu.VMEM(probe.shape, jnp.float32),
            pltpu.VMEM(mats[0].shape, mats[0].dtype),
            pltpu.VMEM(mats[1].shape, mats[1].dtype),
            pltpu.SMEM((info.shape[0],), jnp.int32),
            pltpu.SemaphoreType.DMA((sum(len(parts) for parts in places) + 3,)),
            pltpu.SemaphoreType.DMA((info.shape[0],)),
            pltpu.SemaphoreType.DMA((sum(len(parts) for parts in cuts),)),
        ],
        compiler_params=pltpu.CompilerParams(vmem_limit_bytes=(40 if final else 60) * 1024 * 1024),
        name="frames",
    )(info, *pieces, probe, intensity, *mats)


def shifted(array, axis, by):
    count = lax.axis_size(axis)
    return lax.ppermute(array, axis, [(i, (i + by) % count) for i in range(count)])


def moved(array, axis, by):
    row_count, col_count = lax.axis_size("row"), lax.axis_size("col")
    sizes = {"x": row_count // 2, "z": 4, "y": col_count // 4, "core": 2}
    pairs = []
    for x in range(sizes["x"]):
        for z in range(sizes["z"]):
            for y in range(sizes["y"]):
                for core in range(sizes["core"]):
                    ends = []
                    for step in (0, by):
                        at = {"x": x, "z": z, "y": y, "core": core}
                        at[axis] = (at[axis] + step) % sizes[axis]
                        row = at["x"] * 2 + at["z"] % 2
                        col = (at["z"] // 2) * (col_count // 2) + at["y"] * 2 + at["core"]
                        ends.append(row * col_count + col)
                    pairs.append(tuple(ends))
    return lax.ppermute(array, ("row", "col"), pairs)


def core_and_x():
    return (lax.axis_index("col") % 2, lax.axis_index("row") // 2, lax.axis_size("row") // 2)


def core_share(part):
    core, _, _ = core_and_x()
    halves = part.reshape(2, -1, part.shape[-1])
    mine = lax.dynamic_index_in_dim(halves, core, 0, False)
    other = lax.dynamic_index_in_dim(halves, 1 - core, 0, False)
    return mine + moved(other, "core", 1)


def x_share(half):
    _, x, x_count = core_and_x()
    parts = half.reshape(x_count, -1, half.shape[-1])
    total = lax.dynamic_index_in_dim(parts, x, 0, False)
    arrived = [
        moved(lax.dynamic_index_in_dim(parts, (x + by) % x_count, 0, False), "x", by) for by in range(1, x_count)
    ]
    for value in arrived:
        total = total + value
    return total


def sum_along(total, axis, count):
    for value in [moved(total, axis, by) for by in range(1, count)]:
        total = total + value
    return total


def x_gathered(total):
    _, x, x_count = core_and_x()
    gathered = [total] + [moved(total, "x", by) for by in range(1, x_count)]
    half = jnp.zeros((x_count, *total.shape), jnp.float32)
    for by, value in enumerate(gathered):
        half = lax.dynamic_update_index_in_dim(half, value, (x - by) % x_count, 0)
    return half


def both_halves(half, shape):
    core, _, _ = core_and_x()
    other = moved(half, "core", 1)
    first = jnp.where(core == 0, half, other)
    second = jnp.where(core == 0, other, half)
    return jnp.concatenate([first, second], axis=0).reshape(shape)


def on_device(object_field, probe, intensity, centers, picked):
    tile = object_field.shape[1]
    side = probe.shape[-1]
    width = side // 2
    half = tile // 2
    full = tile + side
    rows_all = tile * lax.axis_size("row")
    cols_all = tile * lax.axis_size("col")
    frames_total = intensity.shape[0] * lax.axis_size("row") * lax.axis_size("col")
    mats = tables(side)
    local_row = (centers[:, 0] - lax.axis_index("row") * tile) % rows_all
    local_col = (centers[:, 1] - lax.axis_index("col") * tile) % cols_all
    info = jnp.stack([local_row, local_col, picked], axis=1)
    low, high, last = width, tile - width, full - width

    def whole(row, col, rows, cols):
        return [((0, 0), (row, col), (rows, cols))]

    def cut(row, col, rows, cols):
        return [((row, col), (0, 0), (rows, cols))]

    def outer(rows):
        return jnp.concatenate([rows[:, :, :width], rows[:, :, high:]], axis=2)

    below_outer = shifted(outer(object_field[:, :width]), "row", -1)
    above_outer = shifted(outer(object_field[:, high:]), "row", 1)
    below_inner = shifted(object_field[:, :width, low:high], "row", -1)
    above_inner = shifted(object_field[:, high:, low:high], "row", 1)
    at_left = shifted(object_field[:, :, high:], "col", 1)
    at_right = shifted(object_field[:, :, :width], "col", -1)
    ends_left = shifted(jnp.concatenate([above_outer[:, :, width:], below_outer[:, :, width:]], axis=1), "col", 1)
    corners = jnp.concatenate([above_outer[:, :, :width], below_outer[:, :, :width]], axis=1)
    corners, above_inner, below_inner, ends_left = lax.optimization_barrier(
        (corners, above_inner, below_inner, ends_left)
    )
    ends_right = shifted(corners, "col", -1)

    def two_columns(row):
        return [((0, 0), (row, width), (width, width)), ((0, width), (row, tile), (width, width))]

    placed = [
        (above_outer, two_columns(0)),
        (above_inner, whole(0, side, width, side)),
        (object_field, whole(width, width, tile, tile)),
        (below_outer, two_columns(last)),
        (below_inner, whole(last, side, width, side)),
        (at_left, whole(width, 0, tile, width)),
        (at_right, whole(width, last, tile, width)),
        (ends_left, [((0, 0), (0, 0), (width, width)), ((width, 0), (last, 0), (width, width))]),
        (ends_right, [((0, 0), (0, last), (width, width)), ((width, 0), (last, last), (width, width))]),
    ]
    both_edges = [((0, width), (0, 0), (full, width)), ((0, tile), (0, width), (full, width))]
    cuts = [
        cut(0, 0, full, width),
        cut(0, last, full, width),
        cut(0, side, side, side),
        cut(tile, side, side, side),
        cut(side, side, side, side),
        both_edges,
    ]
    grad_left, grad_right, inner_top, inner_low, inner_mid, edges, probe_part = frames(
        info, placed, probe, intensity, mats, full, cuts, False
    )

    y_count = lax.axis_size("col") // 4
    inner_up = shifted(inner_top, "row", -1)
    inner_down = shifted(inner_low, "row", 1)
    from_right = shifted(grad_left, "col", -1)
    from_left = shifted(grad_right, "col", 1)
    share = x_share(core_share(probe_part))
    share, from_right, from_left, edges, inner_top, inner_low, inner_mid = lax.optimization_barrier(
        (share, from_right, from_left, edges, inner_top, inner_low, inner_mid)
    )
    edges = edges + jnp.concatenate([from_left, from_right], axis=2)
    edges_up = shifted(edges[:, :side], "row", -1)
    edges_down = shifted(edges[:, tile:], "row", 1)
    share = sum_along(share, "y", y_count)
    share, inner_up, inner_down = lax.optimization_barrier((share, inner_up, inner_down))
    half_sum = x_gathered(sum_along(share, "z", 4))
    old_edges = jnp.concatenate([above_outer, outer(object_field), below_outer], axis=1)
    new_edges = jnp.concatenate(
        [
            old_edges[:, :side] - object_rate * (edges[:, :side] + edges_down),
            old_edges[:, side:tile] - object_rate * edges[:, side:tile],
            old_edges[:, tile:] - object_rate * (edges[:, tile:] + edges_up),
        ],
        axis=1,
    )
    left = shifted(new_edges[:, :, width:], "col", 1)
    right = shifted(new_edges[:, :, :width], "col", -1)
    half_sum, left, right = lax.optimization_barrier((half_sum, left, right))
    probe_total = both_halves(half_sum, probe.shape)
    old_inner = jnp.concatenate([above_inner, object_field[:, :, low:high], below_inner], axis=1)
    new_inner = jnp.concatenate(
        [
            old_inner[:, :side] - object_rate * (inner_top + inner_down),
            old_inner[:, side:tile] - object_rate * inner_mid,
            old_inner[:, tile:] - object_rate * (inner_low + inner_up),
        ],
        axis=1,
    )
    probe_now = probe - probe_gain / frames_total * probe_total

    placed = [
        (left, whole(0, 0, full, width)),
        (right, whole(0, last, full, width)),
        (new_edges, [((0, 0), (0, width), (full, width)), ((0, width), (0, tile), (full, width))]),
        (new_inner, whole(0, side, full, side)),
    ]
    reach = width + half
    cuts = [
        cut(0, 0, reach, reach),
        cut(reach, 0, full - reach, reach),
        cut(0, reach, reach, width),
        cut(0, tile, reach, 2 * width),
        cut(reach, reach, full - reach, full - reach),
    ]
    out_top, out_rest, here_0, here_1, here_rest, probe_part = frames(
        info, placed, probe_now, intensity, mats, full, cuts, True
    )

    up_0 = shifted(here_0, "row", -1)
    got_top = shifted(out_top, "col", -1)
    share = x_share(core_share(probe_part))
    share, got_top, up_0 = lax.optimization_barrier((share, got_top, up_0))
    up_1 = shifted(here_1[:, :, :width] + got_top[:, :, :width], "row", -1)
    up_2 = shifted(here_1[:, :, width:] + got_top[:, :, width : 2 * width], "row", -1)
    up_3 = shifted(got_top[:, :, 2 * width :], "row", -1)
    share = sum_along(share, "y", y_count)
    share, up_1, up_2, out_rest = lax.optimization_barrier((share, up_1, up_2, out_rest))
    got_rest = shifted(out_rest, "col", -1)
    half_sum = x_gathered(sum_along(share, "z", 4))
    half_sum, up_3 = lax.optimization_barrier((half_sum, up_3))
    probe_total = both_halves(half_sum, probe.shape)
    mine = jnp.concatenate(
        [
            here_rest[:, :, :width],
            here_rest[:, :, width : 2 * width] + got_rest[:, :, :width],
            here_rest[:, :, 2 * width :] + got_rest[:, :, width : 2 * width],
            got_rest[:, :, 2 * width :],
        ],
        axis=2,
    )
    got = jnp.concatenate([up_0, up_1, up_2, up_3], axis=2)
    moved = jnp.concatenate(
        [mine[:, :width], mine[:, width:] + got[:, : 2 * width], got[:, 2 * width :]], axis=1
    )
    return (moved, probe_now - probe_gain / frames_total * probe_total)


def solution(mesh):
    in_specs = (
        P(None, "row", "col"),
        P(),
        P(("row", "col"), None, None),
        P(("row", "col"), None),
        P(("row", "col")),
    )
    out_specs = (P(None, "row", "col"), P())
    return jax.shard_map(
        on_device, mesh=mesh, in_specs=in_specs, out_specs=out_specs, check_vma=False
    )
```

```python
import math

import jax
import jax.numpy as jnp
import numpy as np
from jax import lax
from jax.experimental import pallas as pl
from jax.experimental.pallas import tpu as pltpu
from jax.sharding import PartitionSpec as P

ITERS = 2


object_rate = 0.02
probe_gain = 4.0
LANES = 128
SUBLANES = 8
GROUP = 4
STAGGER = 1


def tables(frame_side):
    indices = np.arange(frame_side)
    angle = (indices[:, None] * indices[None, :] % frame_side) * (2.0 * math.pi / frame_side)
    scale = 1.0 / math.sqrt(frame_side)
    real_part = (np.cos(angle) * scale).astype(np.float32).astype(jnp.bfloat16)
    imag_part = (-np.sin(angle) * scale).astype(np.float32).astype(jnp.bfloat16)
    right_mat = np.block([[real_part, imag_part], [-imag_part, real_part]])
    left_mat = np.block([[real_part, -imag_part], [imag_part, real_part]])
    return (jnp.asarray(right_mat), jnp.asarray(left_mat))


def frames_kernel(places, cuts, final, side, info, *refs):
    count, out_count = len(places), len(cuts)
    pieces = refs[:count]
    probe_far, intens, right_far, left_far = refs[count : count + 4]
    outs = refs[count + 4 : count + 4 + out_count]
    probe_grad, region, grad, held, levels, probe, right_mat, left_mat, chosen, in_sems, level_sems, out_sems = refs[
        count + 4 + out_count :
    ]
    arriving = []
    for piece, parts in zip(pieces, places):
        for (row_from, col_from), (row_at, col_at), (rows, cols) in parts:
            arriving.append(
                pltpu.make_async_copy(
                    piece.at[:, row_from : row_from + rows, col_from : col_from + cols],
                    region.at[:, row_at : row_at + rows, col_at : col_at + cols],
                    in_sems.at[len(arriving)],
                )
            )
    for source, target in ((probe_far, probe), (right_far, right_mat), (left_far, left_mat)):
        arriving.append(pltpu.make_async_copy(source, target, in_sems.at[len(arriving)]))
    for copy in arriving:
        copy.start()

    def level_copy(slot):
        return pltpu.make_async_copy(intens.at[slot], levels.at[slot], level_sems.at[slot])

    def pick(slot, found):
        @pl.when(info[slot, 2] != 0)
        def _():
            chosen[found] = slot
            level_copy(slot).start()

        return found + jnp.where(info[slot, 2] != 0, 1, 0)

    total = lax.fori_loop(0, info.shape[0], pick, jnp.int32(0))
    grad[...] = jnp.zeros_like(grad)
    probe_grad[...] = jnp.zeros_like(probe_grad)
    for copy in arriving:
        copy.wait()
    lane = lax.broadcasted_iota(jnp.int32, (side + SUBLANES, LANES), 1)
    line = lax.broadcasted_iota(jnp.int32, (1, SUBLANES, LANES), 1)

    tiles = side // SUBLANES

    def one_group(turns):
        slots = [chosen[jnp.minimum(turn, total - 1)] for turn in turns]
        shares = [jnp.where(turn < total, 1.0, 0.0) for turn in turns]
        places_of = []
        for slot in slots:
            row_at = info[slot, 0]
            col_at = info[slot, 1]
            col_base = pl.multiple_of(col_at // LANES * LANES, LANES)
            row_base = pl.multiple_of(row_at // SUBLANES * SUBLANES, SUBLANES)
            col_shift = col_at - col_base
            row_shift = row_at - row_base
            places_of.append((row_base, col_base, row_shift, col_shift))

        def window(lot, part):
            row_base, col_base, row_shift, col_shift = places_of[lot]
            col_back = jnp.where(col_shift == 0, 0, LANES - col_shift)
            row_back = jnp.where(row_shift == 0, 0, SUBLANES - row_shift)
            inside = lane < LANES - col_shift
            inside_row = line < SUBLANES - row_shift
            rows = pl.ds(row_base, side + SUBLANES)
            turned = [
                pltpu.roll(region[part, rows, pl.ds(pl.multiple_of(col_base + LANES * k, LANES), LANES)], col_back, 1)
                for k in range(3)
            ]
            for k in range(2):
                piece = jnp.where(inside, turned[k], turned[k + 1]).reshape(tiles + 1, SUBLANES, LANES)
                piece = pltpu.roll(piece, row_back, 1)
                piece = jnp.where(inside_row, piece[:tiles], piece[1:]).reshape(side, LANES)
                held[lot, part, :, k * LANES : (k + 1) * LANES] = piece

        def spread(lot, part, value):
            row_base, col_base, row_shift, col_shift = places_of[lot]
            outside = lane >= col_shift
            outside_row = line >= row_shift
            rows = pl.ds(row_base, side + SUBLANES)
            nothing = jnp.zeros((1, SUBLANES, LANES), jnp.float32)
            turned = []
            for k in range(2):
                piece = value[:, k * LANES : (k + 1) * LANES].reshape(tiles, SUBLANES, LANES)
                piece = pltpu.roll(piece, row_shift, 1)
                piece = jnp.where(
                    outside_row,
                    jnp.concatenate([piece, nothing], axis=0),
                    jnp.concatenate([nothing, piece], axis=0),
                ).reshape(side + SUBLANES, LANES)
                turned.append(pltpu.roll(piece, col_shift, 1))
            first, second = turned
            grad[part, rows, pl.ds(col_base, LANES)] += jnp.where(outside, first, 0.0)
            grad[part, rows, pl.ds(pl.multiple_of(col_base + LANES, LANES), LANES)] += jnp.where(outside, second, first)
            grad[part, rows, pl.ds(pl.multiple_of(col_base + 2 * LANES, LANES), LANES)] += jnp.where(outside, 0.0, second)

        lots = range(len(slots))

        def exit_wave(lot):
            window(lot, 0)
            window(lot, 1)
            win_re, win_im = held[lot, 0], held[lot, 1]
            pr_re, pr_im = probe[0], probe[1]
            exit_re = pr_re * win_re - pr_im * win_im
            exit_im = pr_re * win_im + pr_im * win_re
            return jnp.concatenate([exit_re, exit_im], axis=1).astype(jnp.bfloat16)

        def to_wave(flat):
            wave = jnp.dot(flat, right_mat[...], preferred_element_type=jnp.float32).astype(jnp.bfloat16)
            return jnp.concatenate([wave[:, :side], wave[:, side:]], axis=0)

        def to_far(stacked):
            return jnp.dot(left_mat[...], stacked, preferred_element_type=jnp.float32)

        def to_weighted(far, lot):
            far_re, far_im = far[:side], far[side:]
            mismatch = (far_re * far_re + far_im * far_im - levels[slots[lot]]) * shares[lot]
            return jnp.concatenate([mismatch * far_re, mismatch * far_im], axis=0).astype(jnp.bfloat16)

        def to_returned(weighted):
            returned = jnp.dot(right_mat[...], weighted, preferred_element_type=jnp.float32).astype(jnp.bfloat16)
            return jnp.concatenate([returned[:side], returned[side:]], axis=1)

        def to_gradient(flat_back):
            return jnp.dot(flat_back, left_mat[...], preferred_element_type=jnp.float32)

        def add(lot, gradient):
            pr_re, pr_im = probe[0], probe[1]
            gr_re, gr_im = gradient[:, :side], gradient[:, side:]
            win_re, win_im = held[lot, 0], held[lot, 1]
            probe_grad[0] += win_re * gr_re + win_im * gr_im
            probe_grad[1] += win_re * gr_im - win_im * gr_re
            spread(lot, 0, pr_re * gr_re + pr_im * gr_im)
            spread(lot, 1, pr_re * gr_im - pr_im * gr_re)

        for turn, slot in zip(turns, slots):

            @pl.when(turn < total)
            def _(slot=slot):
                level_copy(slot).wait()

        stages = (
            lambda lot, value: exit_wave(lot),
            lambda lot, value: to_wave(value),
            lambda lot, value: to_far(value),
            lambda lot, value: to_weighted(value, lot),
            lambda lot, value: to_returned(value),
            lambda lot, value: to_gradient(value),
            add,
        )
        values = [None] * len(slots)
        for tick in range(len(stages) + STAGGER * (len(slots) - 1)):
            for lot in lots:
                stage = tick - STAGGER * lot
                if 0 <= stage < len(stages):
                    values[lot] = stages[stage](lot, values[lot])

    def one_step(at, carried):
        one_group([GROUP * at + lot for lot in range(GROUP)])
        return carried

    lax.fori_loop(0, (total + GROUP - 1) // GROUP, one_step, 0)
    full = region.shape[1]
    width = side // 2
    if final:
        own = slice(width, full - width)
        for rows, cols in ((slice(0, width), slice(0, full)), (slice(full - width, full), slice(0, full)),
                           (own, slice(0, width)), (own, slice(full - width, full))):
            grad[:, rows, cols] = -object_rate * grad[:, rows, cols]
        grad[:, own, own] = region[:, own, own] - object_rate * grad[:, own, own]
    leaving = []
    for out, parts in zip(outs, cuts):
        for (row_from, col_from), (row_at, col_at), (rows, cols) in parts:
            leaving.append(
                pltpu.make_async_copy(
                    grad.at[:, row_from : row_from + rows, col_from : col_from + cols],
                    out.at[:, row_at : row_at + rows, col_at : col_at + cols],
                    out_sems.at[len(leaving)],
                )
            )
    for copy in leaving:
        copy.start()
    for copy in leaving:
        copy.wait()


def frames(info, placed, probe, intensity, mats, full, cuts, final):
    side = probe.shape[-1]
    vmem = pl.BlockSpec(memory_space=pltpu.VMEM)
    smem = pl.BlockSpec(memory_space=pltpu.SMEM)
    anywhere = pl.BlockSpec(memory_space=pl.ANY)
    far = pl.BlockSpec(memory_space=pltpu.HBM)
    pieces = [piece for piece, parts in placed]
    places = [parts for piece, parts in placed]
    out_shapes = []
    for parts in cuts:
        rows = max(row_at + rows for _, (row_at, _), (rows, _) in parts)
        cols = max(col_at + cols for _, (_, col_at), (_, cols) in parts)
        out_shapes.append(jax.ShapeDtypeStruct((2, rows, cols), jnp.float32))
    out_shapes.append(jax.ShapeDtypeStruct(probe.shape, jnp.float32))

    def kernel(*refs):
        frames_kernel(places, cuts, final, side, *refs)

    return pl.pallas_call(
        kernel,
        out_shape=out_shapes,
        in_specs=[smem] + [anywhere] * len(pieces) + [far] * 4,
        out_specs=[far] * len(cuts) + [vmem],
        scratch_shapes=[
            pltpu.VMEM((2, full, full), jnp.float32),
            pltpu.VMEM((2, full, full), jnp.float32),
            pltpu.VMEM((GROUP, *probe.shape), jnp.float32),
            pltpu.VMEM(intensity.shape, jnp.float32),
            pltpu.VMEM(probe.shape, jnp.float32),
            pltpu.VMEM(mats[0].shape, mats[0].dtype),
            pltpu.VMEM(mats[1].shape, mats[1].dtype),
            pltpu.SMEM((info.shape[0],), jnp.int32),
            pltpu.SemaphoreType.DMA((sum(len(parts) for parts in places) + 3,)),
            pltpu.SemaphoreType.DMA((info.shape[0],)),
            pltpu.SemaphoreType.DMA((sum(len(parts) for parts in cuts),)),
        ],
        compiler_params=pltpu.CompilerParams(vmem_limit_bytes=(40 if final else 60) * 1024 * 1024),
        name="frames",
    )(info, *pieces, probe, intensity, *mats)


def shifted(array, axis, by):
    count = lax.axis_size(axis)
    return lax.ppermute(array, axis, [(i, (i + by) % count) for i in range(count)])


def moved(array, axis, by):
    row_count, col_count = lax.axis_size("row"), lax.axis_size("col")
    sizes = {"x": row_count // 2, "z": 4, "y": col_count // 4, "core": 2}
    pairs = []
    for x in range(sizes["x"]):
        for z in range(sizes["z"]):
            for y in range(sizes["y"]):
                for core in range(sizes["core"]):
                    ends = []
                    for step in (0, by):
                        at = {"x": x, "z": z, "y": y, "core": core}
                        at[axis] = (at[axis] + step) % sizes[axis]
                        row = at["x"] * 2 + at["z"] % 2
                        col = (at["z"] // 2) * (col_count // 2) + at["y"] * 2 + at["core"]
                        ends.append(row * col_count + col)
                    pairs.append(tuple(ends))
    return lax.ppermute(array, ("row", "col"), pairs)


def core_and_x():
    return (lax.axis_index("col") % 2, lax.axis_index("row") // 2, lax.axis_size("row") // 2)


def core_share(part):
    core, _, _ = core_and_x()
    halves = part.reshape(2, -1, part.shape[-1])
    mine = lax.dynamic_index_in_dim(halves, core, 0, False)
    other = lax.dynamic_index_in_dim(halves, 1 - core, 0, False)
    return mine + moved(other, "core", 1)


def x_share(half):
    _, x, x_count = core_and_x()
    parts = half.reshape(x_count, -1, half.shape[-1])
    total = lax.dynamic_index_in_dim(parts, x, 0, False)
    arrived = [
        moved(lax.dynamic_index_in_dim(parts, (x + by) % x_count, 0, False), "x", by) for by in range(1, x_count)
    ]
    for value in arrived:
        total = total + value
    return total


def sum_along(total, axis, count):
    for value in [moved(total, axis, by) for by in range(1, count)]:
        total = total + value
    return total


def x_gathered(total):
    _, x, x_count = core_and_x()
    gathered = [total] + [moved(total, "x", by) for by in range(1, x_count)]
    half = jnp.zeros((x_count, *total.shape), jnp.float32)
    for by, value in enumerate(gathered):
        half = lax.dynamic_update_index_in_dim(half, value, (x - by) % x_count, 0)
    return half


def both_halves(half, shape):
    core, _, _ = core_and_x()
    other = moved(half, "core", 1)
    first = jnp.where(core == 0, half, other)
    second = jnp.where(core == 0, other, half)
    return jnp.concatenate([first, second], axis=0).reshape(shape)


def on_device(object_field, probe, intensity, centers, picked):
    tile = object_field.shape[1]
    side = probe.shape[-1]
    width = side // 2
    half = tile // 2
    full = tile + side
    rows_all = tile * lax.axis_size("row")
    cols_all = tile * lax.axis_size("col")
    frames_total = intensity.shape[0] * lax.axis_size("row") * lax.axis_size("col")
    mats = tables(side)
    local_row = (centers[:, 0] - lax.axis_index("row") * tile) % rows_all
    local_col = (centers[:, 1] - lax.axis_index("col") * tile) % cols_all
    info = jnp.stack([local_row, local_col, picked], axis=1)
    low, high, last = width, tile - width, full - width

    def whole(row, col, rows, cols):
        return [((0, 0), (row, col), (rows, cols))]

    def cut(row, col, rows, cols):
        return [((row, col), (0, 0), (rows, cols))]

    def outer(rows):
        return jnp.concatenate([rows[:, :, :width], rows[:, :, high:]], axis=2)

    below_outer = shifted(outer(object_field[:, :width]), "row", -1)
    above_outer = shifted(outer(object_field[:, high:]), "row", 1)
    below_inner = shifted(object_field[:, :width, low:high], "row", -1)
    above_inner = shifted(object_field[:, high:, low:high], "row", 1)
    at_left = shifted(object_field[:, :, high:], "col", 1)
    at_right = shifted(object_field[:, :, :width], "col", -1)
    ends_left = shifted(jnp.concatenate([above_outer[:, :, width:], below_outer[:, :, width:]], axis=1), "col", 1)
    corners = jnp.concatenate([above_outer[:, :, :width], below_outer[:, :, :width]], axis=1)
    corners, above_inner, below_inner, ends_left = lax.optimization_barrier(
        (corners, above_inner, below_inner, ends_left)
    )
    ends_right = shifted(corners, "col", -1)

    def two_columns(row):
        return [((0, 0), (row, width), (width, width)), ((0, width), (row, tile), (width, width))]

    placed = [
        (above_outer, two_columns(0)),
        (above_inner, whole(0, side, width, side)),
        (object_field, whole(width, width, tile, tile)),
        (below_outer, two_columns(last)),
        (below_inner, whole(last, side, width, side)),
        (at_left, whole(width, 0, tile, width)),
        (at_right, whole(width, last, tile, width)),
        (ends_left, [((0, 0), (0, 0), (width, width)), ((width, 0), (last, 0), (width, width))]),
        (ends_right, [((0, 0), (0, last), (width, width)), ((width, 0), (last, last), (width, width))]),
    ]
    both_edges = [((0, width), (0, 0), (full, width)), ((0, tile), (0, width), (full, width))]
    cuts = [
        cut(0, 0, full, width),
        cut(0, last, full, width),
        cut(0, side, side, side),
        cut(tile, side, side, side),
        cut(side, side, side, side),
        both_edges,
    ]
    grad_left, grad_right, inner_top, inner_low, inner_mid, edges, probe_part = frames(
        info, placed, probe, intensity, mats, full, cuts, False
    )

    y_count = lax.axis_size("col") // 4
    inner_up = shifted(inner_top, "row", -1)
    inner_down = shifted(inner_low, "row", 1)
    from_right = shifted(grad_left, "col", -1)
    from_left = shifted(grad_right, "col", 1)
    share = x_share(core_share(probe_part))
    share, from_right, from_left, edges, inner_top, inner_low, inner_mid = lax.optimization_barrier(
        (share, from_right, from_left, edges, inner_top, inner_low, inner_mid)
    )
    edges = edges + jnp.concatenate([from_left, from_right], axis=2)
    edges_up = shifted(edges[:, :side], "row", -1)
    edges_down = shifted(edges[:, tile:], "row", 1)
    share = sum_along(share, "y", y_count)
    share, inner_up, inner_down = lax.optimization_barrier((share, inner_up, inner_down))
    half_sum = x_gathered(sum_along(share, "z", 4))
    old_edges = jnp.concatenate([above_outer, outer(object_field), below_outer], axis=1)
    new_edges = jnp.concatenate(
        [
            old_edges[:, :side] - object_rate * (edges[:, :side] + edges_down),
            old_edges[:, side:tile] - object_rate * edges[:, side:tile],
            old_edges[:, tile:] - object_rate * (edges[:, tile:] + edges_up),
        ],
        axis=1,
    )
    left = shifted(new_edges[:, :, width:], "col", 1)
    right = shifted(new_edges[:, :, :width], "col", -1)
    half_sum, left, right = lax.optimization_barrier((half_sum, left, right))
    probe_total = both_halves(half_sum, probe.shape)
    old_inner = jnp.concatenate([above_inner, object_field[:, :, low:high], below_inner], axis=1)
    new_inner = jnp.concatenate(
        [
            old_inner[:, :side] - object_rate * (inner_top + inner_down),
            old_inner[:, side:tile] - object_rate * inner_mid,
            old_inner[:, tile:] - object_rate * (inner_low + inner_up),
        ],
        axis=1,
    )
    probe_now = probe - probe_gain / frames_total * probe_total

    placed = [
        (left, whole(0, 0, full, width)),
        (right, whole(0, last, full, width)),
        (new_edges, [((0, 0), (0, width), (full, width)), ((0, width), (0, tile), (full, width))]),
        (new_inner, whole(0, side, full, side)),
    ]
    reach = width + half
    cuts = [
        cut(0, 0, reach, reach),
        cut(reach, 0, full - reach, reach),
        cut(0, reach, reach, width),
        cut(0, tile, reach, 2 * width),
        cut(reach, reach, full - reach, full - reach),
    ]
    out_top, out_rest, here_0, here_1, here_rest, probe_part = frames(
        info, placed, probe_now, intensity, mats, full, cuts, True
    )

    up_0 = shifted(here_0, "row", -1)
    got_top = shifted(out_top, "col", -1)
    share = x_share(core_share(probe_part))
    share, got_top, up_0 = lax.optimization_barrier((share, got_top, up_0))
    up_1 = shifted(here_1[:, :, :width] + got_top[:, :, :width], "row", -1)
    up_2 = shifted(
        jnp.concatenate([here_1[:, :, width:] + got_top[:, :, width : 2 * width], got_top[:, :, 2 * width :]], axis=2),
        "row",
        -1,
    )
    share = sum_along(share, "y", y_count)
    share, up_1, out_rest = lax.optimization_barrier((share, up_1, out_rest))
    got_rest = shifted(out_rest, "col", -1)
    half_sum = x_gathered(sum_along(share, "z", 4))
    half_sum, up_2 = lax.optimization_barrier((half_sum, up_2))
    probe_total = both_halves(half_sum, probe.shape)
    mine = jnp.concatenate(
        [
            here_rest[:, :, :width],
            here_rest[:, :, width : 2 * width] + got_rest[:, :, :width],
            here_rest[:, :, 2 * width :] + got_rest[:, :, width : 2 * width],
            got_rest[:, :, 2 * width :],
        ],
        axis=2,
    )
    got = jnp.concatenate([up_0, up_1, up_2], axis=2)
    moved = jnp.concatenate(
        [mine[:, :width], mine[:, width:] + got[:, : 2 * width], got[:, 2 * width :]], axis=1
    )
    return (moved, probe_now - probe_gain / frames_total * probe_total)


def solution(mesh):
    in_specs = (
        P(None, "row", "col"),
        P(),
        P(("row", "col"), None, None),
        P(("row", "col"), None),
        P(("row", "col")),
    )
    out_specs = (P(None, "row", "col"), P())
    return jax.shard_map(
        on_device, mesh=mesh, in_specs=in_specs, out_specs=out_specs, check_vma=False
    )
```
